256 devices in a mesh: lat: 64 (over z, y, x_hi), lon: 4 (over x_lo, core).
Axes of the slice: x: 4 (x_hi: 2, x_lo: 2; x = x_hi * 2 + x_lo), y: 4, z: 8, core: 2. Of those that a mesh axis runs over, the one named last changes fastest.
Arguments:
- tokens: bfloat16 [192, 256, 512], P('lat', 'lon'), may hold values from -6 to 6
- ocean_count: int32 [192, 4], P('lat', 'lon'), may hold values from 1 to 64
- w_qkv: bfloat16 [512, 1536], replicated, may hold values from -0.25 to 0.25
- w_out: bfloat16 [512, 512], replicated, may hold values from -0.25 to 0.25
- w_up: bfloat16 [512, 1024], replicated, may hold values from -0.25 to 0.25
- w_down: bfloat16 [1024, 512], replicated, may hold values from -0.1875 to 0.1875
- cotangent: bfloat16 [192, 256, 512], P('lat', 'lon'), may hold values from -6 to 6
Outputs:
- block_out: bfloat16 [192, 256, 512], P('lat', 'lon')
- grad_tokens: bfloat16 [192, 256, 512], P('lat', 'lon')
- grad_qkv: float32 [512, 1536], P('lat')
- grad_out: float32 [512, 512], P('lat')
- grad_up: float32 [512, 1024], P('lat')
- grad_down: float32 [1024, 512], P('lat')
The draws below stay inside these ranges and needn't reach their ends.
Inputs may be any that keep to these rules, and one draw needn't show every extreme that they name: The ocean patches of row r in sector s are that sector's first ocean_count[r, s] positions; the others are land.
All inputs are finite; a program needn't handle non-finite values.
Results may differ from the reference program's by a relative error of at most 0.023.
Values may be sent and summed in bfloat16 or wider, within the bound.
No kernel may reach another device: no remote copies, remote signals or barrier semaphores. Data moves between devices by JAX's collectives and lax.ppermute only.
A program may use at most 64 MiB of HBM per device.

```python
import math
import jax
import jax.numpy as jnp
from jax import lax

D = 512
FF = 1024
HEAD_DIM = 64
LON_DEV = 64
ROWS = 192
LON = 256
N_LON = 4


def plant(values, own_key, smallest, largest):
    longest = values.shape.index(max(values.shape))
    spots = []
    for shift in (0, 1):
        where = [jax.random.randint(jax.random.fold_in(own_key, axis), (), 0, length) for axis, length in enumerate(values.shape)]
        where[longest] = (where[longest] + shift) % values.shape[longest]
        spots.append(tuple(where))
    return values.at[spots[0]].set(smallest).at[spots[1]].set(largest)


def shard_levels(rng, extent, pieces, smallest, high):
    def one(position, parts):
        draws = jax.random.uniform(jax.random.fold_in(jax.random.fold_in(rng, 6), position), (parts,), jnp.float32, smallest / len(pieces), high / len(pieces))
        return jnp.repeat(jnp.exp(draws), extent[position] // parts).reshape((-1,) + (1,) * (len(extent) - position - 1))

    level = one(*pieces[0])
    for cut in pieces[1:]:
        level = level * one(*cut)
    return level


def normal_values(stream_key, shape, width, most, split=(), held_as=jnp.bfloat16):
    gain = shard_levels(stream_key, shape, split, -0.22, 0.18) if split else 1.0
    result = jax.random.normal(stream_key, shape, jnp.float32) * width * gain
    return jnp.minimum(jnp.maximum(result, -most), most).astype(held_as)


def setup_inputs(seed: int = 0) -> dict:
    splits = jax.random.split(jax.random.key(seed), 8)
    return {
        "tokens": normal_values(splits[0], (ROWS, LON, D), 1.0, 6.0, ((0, 64), (1, 4))),
        "ocean_count": plant(jax.random.randint(splits[1], (ROWS, N_LON), 1, LON_DEV + 1), jax.random.fold_in(splits[1], 1), 1, LON_DEV).astype(jnp.int32),
        "w_qkv": normal_values(splits[2], (D, 3 * D), D ** -0.5, 0.25),
        "w_out": normal_values(splits[3], (D, D), D ** -0.5, 0.25),
        "w_up": normal_values(splits[4], (D, FF), D ** -0.5, 0.25),
        "w_down": normal_values(splits[5], (FF, D), FF ** -0.5, 0.1875),
        "cotangent": normal_values(splits[6], (ROWS, LON, D), 1.0, 6.0, ((0, 64), (1, 4))),
    }


SOFTMAX_SCALE = 8.0

def widen(values):
    return lax.optimization_barrier(values).astype(jnp.float32)

def elementwise_product(pattern, left_side, right_side):
    return jnp.einsum(pattern, widen(left_side), widen(right_side), precision=lax.Precision.HIGHEST)

def flatten(values):
    return values.reshape(-1, values.shape[-1])

def layer_norm(values):
    average = lax.optimization_barrier(jnp.mean(values, axis=-1, keepdims=True))
    centered = values - average
    variance = lax.optimization_barrier(jnp.mean(centered * centered, axis=-1, keepdims=True))
    return centered * lax.rsqrt(variance + 1e-05)

def split_heads(values, head_count):
    return values.reshape(values.shape[:-1] + (head_count, values.shape[-1] // head_count))

def head_norm(values, head_count):
    shaped = split_heads(values, head_count)
    scaled = shaped * lax.rsqrt(lax.optimization_barrier(jnp.mean(shaped * shaped, axis=-1, keepdims=True)) + 1e-06)
    return scaled.reshape(values.shape)

def project_in(tokens, w_qkv, head_count):
    model_width = tokens.shape[-1]
    normed = layer_norm(tokens.astype(jnp.float32)).astype(jnp.bfloat16)
    projected = elementwise_product('...d,de->...e', normed, w_qkv)
    query_raw = projected[..., :model_width]
    key_raw = projected[..., model_width:2 * model_width]
    query_b = head_norm(query_raw, head_count).astype(jnp.bfloat16)
    key_value = jnp.concatenate([head_norm(key_raw, head_count), projected[..., 2 * model_width:]], axis=-1).astype(jnp.bfloat16)
    return (normed, query_b, key_value, query_raw, key_raw)

def row_scores(query_b, key_value, key_land_mask, head_count):
    model_width = query_b.shape[-1]
    head_features = model_width // head_count
    query_per_head = split_heads(query_b, head_count)
    key_per_head = split_heads(key_value[:, :model_width], head_count)
    unmasked_logits = elementwise_product('mvp,lvp->vml', query_per_head, key_per_head) * (SOFTMAX_SCALE / head_features)
    return jnp.exp(unmasked_logits - SOFTMAX_SCALE) * key_land_mask.astype(jnp.float32)[None, None, :]

def attend_row(query_b, key_value, key_land_mask, head_count):
    model_width = query_b.shape[-1]
    expscore = row_scores(query_b, key_value, key_land_mask, head_count)
    value_heads = split_heads(key_value[:, model_width:], head_count)
    numerator = elementwise_product('hqk,khc->qhc', expscore.astype(jnp.bfloat16), value_heads)
    row_total = jnp.transpose(lax.optimization_barrier(jnp.sum(expscore, axis=-1)))
    return (numerator.reshape(numerator.shape[0], model_width), row_total)

def attend_row_back(query_b, key_value, key_land_mask, row_total, grad_b, gradient_correction, head_count):
    model_width = query_b.shape[-1]
    head_features = model_width // head_count
    expscore = row_scores(query_b, key_value, key_land_mask, head_count)
    row_attention_weight = expscore / jnp.transpose(row_total)[:, :, None]
    query_per_head = split_heads(query_b, head_count)
    key_per_head = split_heads(key_value[:, :model_width], head_count)
    value_heads = split_heads(key_value[:, model_width:], head_count)
    grad_heads = split_heads(grad_b, head_count)
    gradient_weights = elementwise_product('mvp,lvp->vml', grad_heads, value_heads)
    gradient_logits = (row_attention_weight * (gradient_weights - jnp.transpose(gradient_correction)[:, :, None]) * (SOFTMAX_SCALE / head_features)).astype(jnp.bfloat16)
    grad_query = elementwise_product('hqk,khc->qhc', gradient_logits, key_per_head).reshape(-1, model_width)
    grad_key = elementwise_product('hqk,qhc->khc', gradient_logits, query_per_head).reshape(-1, model_width)
    grad_value = elementwise_product('hqk,qhc->khc', row_attention_weight.astype(jnp.bfloat16), grad_heads).reshape(-1, model_width)
    return (grad_query, jnp.concatenate([grad_key, grad_value], axis=-1))

def forward_tail(tokens, attended_b, ocean_mask, w_out, w_up, w_down):
    middle = tokens.astype(jnp.float32) + ocean_mask[..., None] * elementwise_product('...d,de->...e', attended_b, w_out)
    normed_two = layer_norm(middle).astype(jnp.bfloat16)
    lifted = elementwise_product('...d,df->...f', normed_two, w_up)
    active = jax.nn.gelu(lifted).astype(jnp.bfloat16)
    block_out = (middle + ocean_mask[..., None] * elementwise_product('...f,fd->...d', active, w_down)).astype(jnp.bfloat16)
    return (block_out, (middle, normed_two, lifted, active))

def backward_tail(cotangent, ocean_mask, attended_b, tail_saved, w_out, w_up, w_down):
    middle, normed_two, lifted, active = tail_saved
    upstream = cotangent.astype(jnp.float32)
    grad_branch = (ocean_mask[..., None] * upstream).astype(jnp.bfloat16)
    grad_active = elementwise_product('...d,fd->...f', grad_branch, w_down)
    grad_lifted = jax.vjp(jax.nn.gelu, lifted)[1](grad_active)[0].astype(jnp.bfloat16)
    grad_normed = elementwise_product('...f,df->...d', grad_lifted, w_up)
    grad_middle = upstream + jax.vjp(layer_norm, middle)[1](grad_normed)[0]
    grad_attn = (ocean_mask[..., None] * grad_middle).astype(jnp.bfloat16)
    grad_attended = elementwise_product('...e,de->...d', grad_attn, w_out).astype(jnp.bfloat16)
    term_out = elementwise_product('td,te->de', flatten(attended_b), flatten(grad_attn))
    term_up = elementwise_product('td,tf->df', flatten(normed_two), flatten(grad_lifted))
    term_down = elementwise_product('tf,td->fd', flatten(active), flatten(grad_branch))
    return (grad_middle, grad_attended, (term_out, term_up, term_down))

def backward_head(tokens, normed, query_raw, key_raw, grad_query, grad_kv, grad_middle, w_qkv, head_count):
    model_width = tokens.shape[-1]
    grad_qraw = jax.vjp(lambda values: head_norm(values, head_count), query_raw)[1](grad_query)[0]
    grad_kraw = jax.vjp(lambda values: head_norm(values, head_count), key_raw)[1](grad_kv[..., :model_width])[0]
    grad_projected = jnp.concatenate([grad_qraw, grad_kraw, grad_kv[..., model_width:]], axis=-1).astype(jnp.bfloat16)
    term_qkv = elementwise_product('td,te->de', flatten(normed), flatten(grad_projected))
    grad_normed = elementwise_product('...e,de->...d', grad_projected, w_qkv)
    grad_layer = jax.vjp(layer_norm, tokens.astype(jnp.float32))[1](grad_normed)[0]
    return ((grad_middle + grad_layer).astype(jnp.bfloat16), term_qkv)

def reference(tokens, ocean_count, w_qkv, w_out, w_up, w_down, cotangent):
    head_count = D // HEAD_DIM
    positions = jnp.arange(LON, dtype=jnp.int32)
    grad_scale = 1.0 / math.sqrt(ROWS * LON)

    def one_row(weight_sums, row_inputs):
        row_tokens, row_count, row_grad = row_inputs
        sector_count = jnp.take(row_count, (positions // LON_DEV).astype(jnp.int32))
        ocean_mask = (positions % LON_DEV < sector_count).astype(jnp.float32)
        key_land_mask = ocean_mask.astype(jnp.bfloat16)
        normed, query_b, key_value, query_raw, key_raw = project_in(row_tokens, w_qkv, head_count)
        numerator, row_total = attend_row(query_b, key_value, key_land_mask, head_count)
        attended = (split_heads(numerator, head_count) / row_total[:, :, None]).reshape(LON, D)
        attended_b = attended.astype(jnp.bfloat16)
        block_row, tail_saved = forward_tail(row_tokens, attended_b, ocean_mask, w_out, w_up, w_down)
        grad_middle, grad_attended, tail_terms = backward_tail(row_grad, ocean_mask, attended_b, tail_saved, w_out, w_up, w_down)
        gradient_correction = lax.optimization_barrier(jnp.sum(split_heads(widen(grad_attended) * attended, head_count), axis=-1))
        query_parts = []
        grad_kv = jnp.zeros((LON, 2 * D), jnp.float32)
        for sector in range(N_LON):
            first_pos = sector * LON_DEV
            part_query, part_kv = attend_row_back(query_b[first_pos:first_pos + LON_DEV], key_value, key_land_mask, row_total[first_pos:first_pos + LON_DEV], grad_attended[first_pos:first_pos + LON_DEV], gradient_correction[first_pos:first_pos + LON_DEV], head_count)
            query_parts.append(part_query)
            grad_kv = grad_kv + widen(part_kv.astype(jnp.bfloat16))
        grad_query = jnp.concatenate(query_parts, axis=0)
        grad_row, term_qkv = backward_head(row_tokens, normed, query_raw, key_raw, grad_query, grad_kv, grad_middle, w_qkv, head_count)
        new_sums = (weight_sums[0] + term_qkv, weight_sums[1] + tail_terms[0], weight_sums[2] + tail_terms[1], weight_sums[3] + tail_terms[2])
        return (new_sums, (block_row, grad_row))
    start_sums = (jnp.zeros((D, 3 * D), jnp.float32), jnp.zeros((D, D), jnp.float32), jnp.zeros((D, FF), jnp.float32), jnp.zeros((FF, D), jnp.float32))
    weight_sums, row_outputs = lax.scan(one_row, start_sums, (tokens, ocean_count, cotangent))
    block_out, grad_tokens = row_outputs
    return (block_out, grad_tokens, weight_sums[0] * grad_scale, weight_sums[1] * grad_scale, weight_sums[2] * grad_scale, weight_sums[3] * grad_scale)
```

```python
import math

import jax
import jax.numpy as jnp
from jax import lax
from jax.sharding import PartitionSpec as P

HEAD_DIM = 64


SOFTMAX_SCALE = 8.0


def widen(values):
    return lax.optimization_barrier(values).astype(jnp.float32)


def elementwise_product(pattern, left_side, right_side):
    return jnp.einsum(pattern, left_side, right_side, preferred_element_type=jnp.float32)


def flatten(values):
    return values.reshape(-1, values.shape[-1])


def layer_norm(values):
    average = jnp.mean(values, axis=-1, keepdims=True)
    centered = values - average
    variance = jnp.mean(centered * centered, axis=-1, keepdims=True)
    return centered * lax.rsqrt(variance + 1e-05)


def split_heads(values, head_count):
    return values.reshape(values.shape[:-1] + (head_count, values.shape[-1] // head_count))


def head_norm(values, head_count):
    shaped = split_heads(values, head_count)
    scaled = shaped * lax.rsqrt(jnp.mean(shaped * shaped, axis=-1, keepdims=True) + 1e-06)
    return scaled.reshape(values.shape)


def project_in(tokens, w_qkv, head_count):
    model_width = tokens.shape[-1]
    normed = layer_norm(tokens.astype(jnp.float32)).astype(jnp.bfloat16)
    projected = elementwise_product("...d,de->...e", normed, w_qkv)
    query_raw = projected[..., :model_width]
    key_raw = projected[..., model_width : 2 * model_width]
    query_b = head_norm(query_raw, head_count).astype(jnp.bfloat16)
    key_value = jnp.concatenate(
        [head_norm(key_raw, head_count), projected[..., 2 * model_width :]], axis=-1
    ).astype(jnp.bfloat16)
    return (normed, query_b, key_value, query_raw, key_raw)


def forward_tail(tokens, attended_b, ocean_mask, w_out, w_up, w_down):
    middle = tokens.astype(jnp.float32) + ocean_mask[..., None] * elementwise_product(
        "...d,de->...e", attended_b, w_out
    )
    normed_two = layer_norm(middle).astype(jnp.bfloat16)
    lifted = elementwise_product("...d,df->...f", normed_two, w_up)
    active = jax.nn.gelu(lifted).astype(jnp.bfloat16)
    block_out = (
        middle + ocean_mask[..., None] * elementwise_product("...f,fd->...d", active, w_down)
    ).astype(jnp.bfloat16)
    return (block_out, (middle, normed_two, lifted, active))


def backward_tail(cotangent, ocean_mask, attended_b, tail_saved, w_out, w_up, w_down):
    middle, normed_two, lifted, active = tail_saved
    upstream = cotangent.astype(jnp.float32)
    grad_branch = (ocean_mask[..., None] * upstream).astype(jnp.bfloat16)
    grad_active = elementwise_product("...d,fd->...f", grad_branch, w_down)
    grad_lifted = jax.vjp(jax.nn.gelu, lifted)[1](grad_active)[0].astype(jnp.bfloat16)
    grad_normed = elementwise_product("...f,df->...d", grad_lifted, w_up)
    grad_middle = upstream + jax.vjp(layer_norm, middle)[1](grad_normed)[0]
    grad_attn = (ocean_mask[..., None] * grad_middle).astype(jnp.bfloat16)
    grad_attended = elementwise_product("...e,de->...d", grad_attn, w_out).astype(jnp.bfloat16)
    term_out = elementwise_product("td,te->de", flatten(attended_b), flatten(grad_attn))
    term_up = elementwise_product("td,tf->df", flatten(normed_two), flatten(grad_lifted))
    term_down = elementwise_product("tf,td->fd", flatten(active), flatten(grad_branch))
    return (grad_middle, grad_attended, (term_out, term_up, term_down))


def lat_index(z, y, x_hi):
    return (z * 4 + y) * 2 + x_hi


CORE = [(0, 1), (1, 0), (2, 3), (3, 2)]
X_LO = [(0, 2), (2, 0), (1, 3), (3, 1)]
Z_GROUPS = [[lat_index(z, y, x) for z in range(8)] for y in range(4) for x in range(2)]
PLANE_GROUPS = [
    [lat_index(z, y, x_hi) * 4 + x_lo * 2 + core for y in range(4) for x_hi in range(2) for x_lo in range(2)]
    for z in range(8)
    for core in range(2)
]


def gather_sectors(values):
    from_core = lax.ppermute(values, "lon", CORE)
    from_x = lax.ppermute(values, "lon", X_LO)
    return (values, from_core, from_x, lax.ppermute(from_x, "lon", CORE))


def scatter_sectors(own, parts):
    for_core = jnp.stack([parts[0], parts[2]])
    from_core = lax.ppermute(for_core, "lon", CORE).astype(jnp.float32)
    for_x = (parts[1].astype(jnp.float32) + from_core[1]).astype(jnp.bfloat16)
    return own + from_core[0] + lax.ppermute(for_x, "lon", X_LO).astype(jnp.float32)


def quarters(term):
    width = term.shape[1] // 4
    return term.reshape(8, 4, 2, 8, 2, 2, width).transpose(1, 2, 4, 0, 3, 5, 6)


def reduce_weights(terms):
    term_qkv, term_out, term_up, term_down = terms
    down_rows = term_down.reshape(64, 2, 8, 512).transpose(0, 2, 1, 3).reshape(512, 1024)
    stacked = jnp.concatenate(
        [quarters(term.astype(jnp.bfloat16)) for term in (term_qkv, term_out, term_up, down_rows)], axis=-1
    )
    core = lax.axis_index("lon") % 2
    keep = lax.dynamic_index_in_dim(stacked, core, 5, keepdims=False)
    send = lax.dynamic_index_in_dim(stacked, 1 - core, 5, keepdims=False)
    half = keep.astype(jnp.float32) + lax.ppermute(send, "lon", CORE).astype(jnp.float32)
    half = half.astype(jnp.bfloat16).reshape(16 * 64, 1024)
    plane = lax.all_to_all(half, ("lat", "lon"), 0, 0, axis_index_groups=PLANE_GROUPS, tiled=True)
    plane = jnp.sum(plane.reshape(16, 64, 1024).astype(jnp.float32), axis=0).astype(jnp.bfloat16)
    column = lax.all_to_all(plane, "lat", 0, 0, axis_index_groups=Z_GROUPS, tiled=True)
    column = jnp.sum(column.reshape(8, 8, 1024).astype(jnp.float32), axis=0).astype(jnp.bfloat16)
    whole = lax.all_gather(column, "lon", axis=0)
    scale = 1.0 / math.sqrt(64 * 4 * 192)
    whole = whole.astype(jnp.float32) * scale
    pick = lambda lo, hi: whole[:, :, lo:hi].transpose(1, 0, 2).reshape(8, -1)
    down = pick(768, 1024).reshape(8, 2, 512).transpose(1, 0, 2).reshape(16, 512)
    return (pick(0, 384), pick(384, 512), pick(512, 768), down)


def local(tokens, ocean_count, w_qkv, w_out, w_up, w_down, cotangent):
    band_rows, local_len, model_width = tokens.shape
    head_count = model_width // HEAD_DIM
    bf = jnp.bfloat16
    tokens_all = jnp.stack(gather_sectors(tokens))
    counts_all = jnp.stack(gather_sectors(ocean_count))
    masks_all = (
        lax.broadcasted_iota(jnp.int32, (4, band_rows, local_len), 2) < counts_all
    ).astype(jnp.float32)
    ocean_mask = masks_all[0]
    normed_all = layer_norm(tokens_all.astype(jnp.float32)).astype(bf)
    normed = normed_all[0]
    query_raw = elementwise_product("rpd,de->rpe", normed, w_qkv[:, :512])
    kv_raw = elementwise_product("srpd,de->srpe", normed_all, w_qkv[:, 512:])
    key_raw = kv_raw[..., :512]
    query_b = head_norm(query_raw, head_count).astype(bf)
    query_h = split_heads(query_b, head_count)
    key_h = split_heads(head_norm(key_raw, head_count).astype(bf), head_count)
    value_h = split_heads(kv_raw[..., 512:].astype(bf), head_count)
    logits = elementwise_product("rphc,srqhc->rhpsq", query_h, key_h) * (SOFTMAX_SCALE / HEAD_DIM)
    key_mask = masks_all.transpose(1, 0, 2)[:, None, None]
    expscore = jnp.exp(logits - SOFTMAX_SCALE) * key_mask
    row_total = jnp.sum(expscore, axis=(3, 4))
    numerator = elementwise_product("rhpsq,srqhc->rphc", expscore.astype(bf), value_h)
    attended_h = numerator / row_total.transpose(0, 2, 1)[..., None]
    attended = attended_h.reshape(tokens.shape)
    attended_b = attended.astype(bf)
    block_out, tail_saved = forward_tail(tokens, attended_b, ocean_mask, w_out, w_up, w_down)
    grad_middle, grad_attended, tail_terms = backward_tail(
        cotangent, ocean_mask, attended_b, tail_saved, w_out, w_up, w_down
    )
    grad_h = split_heads(grad_attended, head_count)
    delta = jnp.sum(grad_h.astype(jnp.float32) * attended_h, axis=-1).transpose(0, 2, 1)
    weight = expscore / row_total[..., None, None]
    grad_weight = elementwise_product("rphc,srqhc->rhpsq", grad_h, value_h)
    grad_logits = (weight * (grad_weight - delta[..., None, None]) * (SOFTMAX_SCALE / HEAD_DIM)).astype(bf)
    grad_query = elementwise_product("rhpsq,srqhc->rphc", grad_logits, key_h).reshape(tokens.shape)
    grad_key = elementwise_product("rhpsq,rphc->srqhc", grad_logits, query_h).reshape(key_raw.shape)
    grad_value = elementwise_product("rhpsq,rphc->srqhc", weight.astype(bf), grad_h).reshape(key_raw.shape)
    norm_back = lambda raw, grad: jax.vjp(lambda values: head_norm(values, head_count), raw)[1](grad)[0]
    grad_q = norm_back(query_raw, grad_query).astype(bf)
    grad_kv = jnp.concatenate([norm_back(key_raw, grad_key), grad_value], axis=-1).astype(bf)
    term_qkv = jnp.concatenate(
        [
            elementwise_product("rpd,rpe->de", normed, grad_q),
            elementwise_product("srpd,srpe->de", normed_all, grad_kv),
        ],
        axis=-1,
    )
    normed_parts = elementwise_product("srpe,de->srpd", grad_kv, w_qkv[:, 512:])
    grad_own = normed_parts[0] + elementwise_product("rpe,de->rpd", grad_q, w_qkv[:, :512])
    others = normed_parts[1:].astype(bf)
    grad_normed = scatter_sectors(grad_own, others)
    grad_layer = jax.vjp(layer_norm, tokens.astype(jnp.float32))[1](grad_normed)[0]
    grad_tokens = (grad_middle + grad_layer).astype(bf)
    return (block_out, grad_tokens) + reduce_weights((term_qkv,) + tail_terms)


def solution(mesh):
    in_specs = (P("lat", "lon", None), P("lat", "lon"), P(), P(), P(), P(), P("lat", "lon", None))
    out_specs = (
        P("lat", "lon", None),
        P("lat", "lon", None),
        P("lat", None),
        P("lat", None),
        P("lat", None),
        P("lat", None),
    )
    return jax.shard_map(local, mesh=mesh, in_specs=in_specs, out_specs=out_specs, check_vma=False)
```

```python
import math

import jax
import jax.numpy as jnp
from jax import lax
from jax.experimental import pallas as pl
from jax.experimental.pallas import tpu as pltpu
from jax.sharding import PartitionSpec as P

F32 = jnp.float32
BF16 = jnp.bfloat16
HEAD_DIM = 64
SOFTMAX_SCALE = 8.0
WIDTH = 512
HIDDEN = 1024
ROWS_DEV = 3
SECTOR = 64
TOKENS = ROWS_DEV * SECTOR
KEYS = 4 * SECTOR
GROUP = 256
GELU_A = math.sqrt(2.0 / math.pi)
GELU_B = 0.044715
NEAR_MB = 20
FRONT_MB = 28
BACK_MB = 28


def lat_index(z, y, x_hi):
    return (z * 4 + y) * 2 + x_hi


CORE = [(0, 1), (1, 0), (2, 3), (3, 2)]
X_LO = [(0, 2), (2, 0), (1, 3), (3, 1)]
Z_GROUPS = [[lat_index(z, y, x) for z in range(8)] for y in range(4) for x in range(2)]
PLANE_GROUPS = [
    [lat_index(z, y, x_hi) * 4 + x_lo * 2 + core for y in range(4) for x_hi in range(2) for x_lo in range(2)]
    for z in range(8)
    for core in range(2)
]


def mm(left, right):
    return lax.dot_general(left, right, (((1,), (0,)), ((), ())), preferred_element_type=F32)


def mm_nt(left, right):
    return lax.dot_general(left, right, (((1,), (1,)), ((), ())), preferred_element_type=F32)


def mm_tn(left, right):
    return lax.dot_general(left, right, (((0,), (0,)), ((), ())), preferred_element_type=F32)


def mean_last(values):
    return jnp.sum(values, axis=-1, keepdims=True) * (1.0 / values.shape[-1])


def layer_norm(values):
    centered = values - mean_last(values)
    inverse = lax.rsqrt(mean_last(centered * centered) + 1e-05)
    return centered * inverse, inverse


def layer_norm_back(normed, inverse, grad):
    return inverse * (grad - mean_last(grad) - normed * mean_last(grad * normed))


def head_blocks():
    same = lax.broadcasted_iota(jnp.int32, (GROUP, GROUP), 0) // HEAD_DIM == (
        lax.broadcasted_iota(jnp.int32, (GROUP, GROUP), 1) // HEAD_DIM
    )
    return jnp.where(same, 1.0, 0.0).astype(BF16)


def head_mean(values, blocks):
    parts = [
        mm(values[:, at : at + GROUP].astype(BF16), blocks) for at in range(0, values.shape[1], GROUP)
    ]
    return (parts[0] if len(parts) == 1 else jnp.concatenate(parts, axis=1)) * (1.0 / HEAD_DIM)


def head_masks(dtype):
    lane = lax.broadcasted_iota(jnp.int32, (1, GROUP), 1) // HEAD_DIM
    return [jnp.where(lane == head, 1.0, 0.0).astype(dtype) for head in range(4)]


def stack_heads(values, masks):
    return jnp.concatenate([values * mask for mask in masks], axis=0)


def unstack_heads(values, masks):
    return sum(values[head * SECTOR : (head + 1) * SECTOR] * masks[head] for head in range(4))


def store_pieces(out_ref, x_lo, column, product):
    width = product.shape[1]
    split = product.reshape(8, 8, 8, width)
    for place in range(8):
        piece = jnp.concatenate([split[z, place] for z in range(8)], axis=0)
        out_ref[place * 2 + x_lo, :, column : column + width] = piece.astype(BF16)


def rows_of(row, width=SECTOR):
    return slice(row * width, (row + 1) * width)


def key_value(tok_ref, w_qkv_ref, blocks, slot, slots, normed_ref, key_ref, value_ref, inv_k_ref):
    normed = layer_norm(tok_ref[...].astype(F32))[0].astype(BF16)
    key_raw = mm(normed, w_qkv_ref[:, WIDTH : 2 * WIDTH])
    inv_k = lax.rsqrt(head_mean(key_raw * key_raw, blocks) + 1e-06)
    key_b = (key_raw * inv_k).astype(BF16)
    inv_kb = inv_k.astype(BF16)
    value_b = mm(normed, w_qkv_ref[:, 2 * WIDTH :]).astype(BF16)
    for row in range(ROWS_DEV):
        at = (row * slots + slot) * SECTOR
        for ref, val in (
            (normed_ref, normed),
            (key_ref, key_b),
            (inv_k_ref, inv_kb),
            (value_ref, value_b),
        ):
            ref[at : at + SECTOR, :] = val[rows_of(row)]
    return normed


def own_mask(count_ref):
    place = lax.broadcasted_iota(jnp.int32, (SECTOR, 1), 0)
    return jnp.concatenate(
        [jnp.where(place < count_ref[row, 0], 1.0, 0.0) for row in range(ROWS_DEV)], axis=0
    )


def near_kernel(
    count_ref,
    tok0_ref,
    w_qkv_ref,
    w_down_ref,
    cot_ref,
    normed_ref,
    key_ref,
    value_ref,
    inv_k_ref,
    query_ref,
    inv_q_ref,
    grad_active_ref,
):
    blocks = head_blocks()
    normed = key_value(tok0_ref, w_qkv_ref, blocks, 0, 1, normed_ref, key_ref, value_ref, inv_k_ref)
    query_raw = mm(normed, w_qkv_ref[:, :WIDTH])
    inv_q = lax.rsqrt(head_mean(query_raw * query_raw, blocks) + 1e-06)
    inv_q_ref[...] = inv_q.astype(BF16)
    query_ref[...] = (query_raw * inv_q).astype(BF16)
    branch = (own_mask(count_ref) * cot_ref[...].astype(F32)).astype(BF16)
    grad_active_ref[...] = mm_nt(branch, w_down_ref[...]).astype(BF16)


def mate_kernel(tok1_ref, w_qkv_ref, normed_ref, key_ref, value_ref, inv_k_ref):
    key_value(tok1_ref, w_qkv_ref, head_blocks(), 0, 1, normed_ref, key_ref, value_ref, inv_k_ref)


def row_join(row, lanes, own_ref, mate_ref, far_ref):
    own = rows_of(row)
    return jnp.concatenate(
        [own_ref[own, lanes], mate_ref[own, lanes], far_ref[rows_of(row, 2 * SECTOR), lanes]], axis=0
    )


def front_kernel(
    core_ref,
    count_ref,
    count1_ref,
    count2_ref,
    count3_ref,
    tok0_ref,
    tok2_ref,
    tok3_ref,
    w_qkv_ref,
    w_out_ref,
    w_up_ref,
    w_down_ref,
    cot_ref,
    query_ref,
    own_key_ref,
    own_value_ref,
    mate_key_ref,
    mate_value_ref,
    grad_active_ref,
    block_out_ref,
    keep_ref,
    send_ref,
    grad_middle_ref,
    normed_ref,
    key_ref,
    value_ref,
    inv_k_ref,
    probs_ref,
    grad_att_ref,
    att_ref,
    lift_ref,
    attn_ref,
    branch_ref,
):
    blocks = head_blocks()
    masks_b = head_masks(BF16)
    masks_f = head_masks(F32)
    core = core_ref[0]
    key_value(tok2_ref, w_qkv_ref, blocks, 0, 2, normed_ref, key_ref, value_ref, inv_k_ref)
    key_value(tok3_ref, w_qkv_ref, blocks, 1, 2, normed_ref, key_ref, value_ref, inv_k_ref)

    key_place = lax.broadcasted_iota(jnp.int32, (1, KEYS), 1)
    for row in range(ROWS_DEV):
        limit = jnp.zeros((1, KEYS), jnp.int32)
        for sector, ref in enumerate((count_ref, count1_ref, count2_ref, count3_ref)):
            limit = jnp.where(key_place // SECTOR == sector, ref[row, 0], limit)
        key_mask = jnp.where(key_place % SECTOR < limit, 1.0, 0.0)
        for group in range(2):
            lanes = slice(group * GROUP, (group + 1) * GROUP)
            stacked = stack_heads(query_ref[rows_of(row), lanes], masks_b)
            keys = row_join(row, lanes, own_key_ref, mate_key_ref, key_ref)
            values = row_join(row, lanes, own_value_ref, mate_value_ref, value_ref)
            scores = mm_nt(stacked, keys)
            expscore = jnp.exp(scores * (SOFTMAX_SCALE / HEAD_DIM) - SOFTMAX_SCALE) * key_mask
            total = jnp.sum(expscore, axis=1, keepdims=True)
            probs = (expscore * (1.0 / total)).astype(BF16)
            probs_ref[row * 2 + group] = probs
            att_ref[rows_of(row), lanes] = unstack_heads(mm(probs, values), masks_f).astype(BF16)

    mask = own_mask(count_ref)
    attended = att_ref[...]
    middle = tok0_ref[...].astype(F32) + mask * mm(attended, w_out_ref[...])
    normed_two, inverse = layer_norm(middle)
    normed_two_b = normed_two.astype(BF16)
    lifted = mm(normed_two_b, w_up_ref[...])
    square = lifted * lifted
    bent = jnp.tanh(GELU_A * lifted * (1.0 + GELU_B * square))
    half = 0.5 * (1.0 + bent)
    active = (lifted * half).astype(BF16)
    slope = half + 0.5 * lifted * (1.0 - bent * bent) * (GELU_A * (1.0 + 3.0 * GELU_B * square))
    block_out_ref[...] = (middle + mask * mm(active, w_down_ref[...])).astype(BF16)
    upstream = cot_ref[...].astype(F32)
    branch = (mask * upstream).astype(BF16)
    grad_lifted = (slope * grad_active_ref[...].astype(F32)).astype(BF16)
    grad_normed = mm_nt(grad_lifted, w_up_ref[...])
    grad_middle = upstream + layer_norm_back(normed_two, inverse, grad_normed)
    grad_middle_ref[...] = grad_middle
    grad_attn = (mask * grad_middle).astype(BF16)
    grad_att_ref[...] = mm_nt(grad_attn, w_out_ref[...]).astype(BF16)

    for part in range(4):
        lift_ref[part] = grad_lifted[:, part * 256 : (part + 1) * 256]
        attn_ref[part] = grad_attn[:, part * 128 : (part + 1) * 128]
    for part in range(2):
        branch_ref[part] = branch[:, part * 256 : (part + 1) * 256]
    for out_ref, half_index in ((keep_ref, core), (send_ref, 1 - core)):
        pair = jnp.concatenate([attn_ref[half_index], attn_ref[half_index + 2]], axis=1)
        term_out = mm_tn(attended, pair)
        for x_lo in range(2):
            store_pieces(out_ref, x_lo, 0, term_out[:, x_lo * 128 : (x_lo + 1) * 128])
            store_pieces(out_ref, x_lo, 128, mm_tn(normed_two_b, lift_ref[half_index + 2 * x_lo]))
        term_down = mm_tn(active, branch_ref[half_index]).reshape(64, 2, 8, 256)
        for x_lo in range(2):
            store_pieces(out_ref, x_lo, 384, term_down[:, x_lo].reshape(512, 256))


def norm_back(normed_b, inverse_b, grad, blocks):
    normed = normed_b.astype(F32)
    shift = head_mean(normed * grad, blocks)
    return (inverse_b.astype(F32) * (grad - normed * shift)).astype(BF16)


def back_kernel(
    core_ref,
    query_ref,
    inv_q_ref,
    own_normed_ref,
    own_key_ref,
    own_value_ref,
    own_inv_k_ref,
    mate_normed_ref,
    mate_key_ref,
    mate_value_ref,
    mate_inv_k_ref,
    normed_ref,
    key_ref,
    value_ref,
    inv_k_ref,
    probs_ref,
    grad_att_ref,
    keep_ref,
    send_ref,
    gq_ref,
    gk_ref,
    gv_ref,
):
    blocks = head_blocks()
    masks_b = head_masks(BF16)
    masks_f = head_masks(F32)
    core = core_ref[0]
    for row in range(ROWS_DEV):
        own = rows_of(row)
        mate = slice(own.start + TOKENS, own.stop + TOKENS)
        far = rows_of(row, 2 * SECTOR)
        far = slice(far.start + 2 * TOKENS, far.stop + 2 * TOKENS)
        for group in range(2):
            lanes = slice(group * GROUP, (group + 1) * GROUP)
            keys = row_join(row, lanes, own_key_ref, mate_key_ref, key_ref)
            values = row_join(row, lanes, own_value_ref, mate_value_ref, value_ref)
            inv_k = row_join(row, lanes, own_inv_k_ref, mate_inv_k_ref, inv_k_ref)
            stacked_q = stack_heads(query_ref[own, lanes], masks_b)
            stacked_g = stack_heads(grad_att_ref[own, lanes], masks_b)
            probs_b = probs_ref[row * 2 + group]
            probs = probs_b.astype(F32)
            grad_probs = mm_nt(stacked_g, values)
            delta = jnp.sum(probs * grad_probs, axis=1, keepdims=True)
            grad_scores = (probs * (grad_probs - delta) * (SOFTMAX_SCALE / HEAD_DIM)).astype(BF16)
            grad_q = unstack_heads(mm(grad_scores, keys), masks_f)
            grad_k = mm_tn(grad_scores, stacked_q)
            grad_v = mm_tn(probs_b, stacked_g).astype(BF16)
            grad_q = norm_back(query_ref[own, lanes], inv_q_ref[own, lanes], grad_q, blocks)
            grad_k = norm_back(keys, inv_k, grad_k, blocks)
            for part in range(2):
                at = slice(part * 128, (part + 1) * 128)
                gq_ref[group * 2 + part, own, :] = grad_q[:, at]
                for ref, grad in ((gk_ref, grad_k), (gv_ref, grad_v)):
                    ref[group * 2 + part, own, :] = grad[:SECTOR, at]
                    ref[group * 2 + part, mate, :] = grad[SECTOR : 2 * SECTOR, at]
                    ref[group * 2 + part, far, :] = grad[2 * SECTOR :, at]

    normed_all = jnp.concatenate([own_normed_ref[...], mate_normed_ref[...], normed_ref[...]], axis=0)
    for out_ref, half_index in ((keep_ref, core), (send_ref, 1 - core)):
        pair = jnp.concatenate([gq_ref[half_index], gq_ref[half_index + 2]], axis=1)
        term_q = mm_tn(own_normed_ref[...], pair)
        for x_lo in range(2):
            store_pieces(out_ref, x_lo, 0, term_q[:, x_lo * 128 : (x_lo + 1) * 128])
            pair = jnp.concatenate([gk_ref[half_index + 2 * x_lo], gv_ref[half_index + 2 * x_lo]], axis=1)
            store_pieces(out_ref, x_lo, 128, mm_tn(normed_all, pair))


def push_kernel(w_qkv_ref, gq_ref, gk_ref, gv_ref, for_core_ref, for_x_ref, own_ref):
    grad_q = jnp.concatenate([gq_ref[part] for part in range(4)], axis=1)

    def grad_normed(rows):
        grads = [ref[part, rows, :] for ref in (gk_ref, gv_ref) for part in range(4)]
        return mm_nt(jnp.concatenate(grads, axis=1), w_qkv_ref[:, WIDTH:])

    for_core_ref[0] = grad_normed(slice(TOKENS, 2 * TOKENS)).astype(BF16)
    far = grad_normed(slice(2 * TOKENS, 4 * TOKENS)).astype(BF16)
    for row in range(ROWS_DEV):
        at = row * 2 * SECTOR
        for_x_ref[rows_of(row), :] = far[at : at + SECTOR]
        for_core_ref[1, rows_of(row), :] = far[at + SECTOR : at + 2 * SECTOR]
    own_ref[...] = grad_normed(slice(0, TOKENS)) + mm_nt(grad_q, w_qkv_ref[:, :WIDTH])


def join_kernel(keep1_ref, recv1_ref, keep2_ref, recv2_ref, out_ref):
    for piece in range(16):
        out_ref[piece, :, :384] = (keep2_ref[piece].astype(F32) + recv2_ref[piece].astype(F32)).astype(BF16)
        out_ref[piece, :, 384:] = (keep1_ref[piece].astype(F32) + recv1_ref[piece].astype(F32)).astype(BF16)


def final_kernel(whole_ref, qkv_ref, out_ref, up_ref, down_ref):
    whole = whole_ref[...].astype(F32) * (1.0 / math.sqrt(64 * 4 * TOKENS))
    for quarter in range(4):
        part = whole[quarter * 8 : (quarter + 1) * 8]
        at = slice(quarter * 128, (quarter + 1) * 128)
        for matrix in range(3):
            low = matrix * WIDTH + quarter * 128
            qkv_ref[:, low : low + 128] = part[:, matrix * 128 : (matrix + 1) * 128]
        out_ref[:, at] = part[:, 384:512]
        up_ref[:, quarter * 256 : (quarter + 1) * 256] = part[:, 512:768]
        side = (quarter % 2) * 256
        down_ref[(quarter // 2) * 8 : (quarter // 2) * 8 + 8, side : side + 256] = part[:, 768:]


def vmem(count):
    return [pl.BlockSpec(memory_space=pltpu.VMEM)] * count


def smem(count):
    return [pl.BlockSpec(memory_space=pltpu.SMEM)] * count


def shape(dims, dtype):
    return jax.ShapeDtypeStruct(dims, dtype)


TOKEN = (TOKENS, WIDTH)
PAIR = (2 * TOKENS, WIDTH)


def params(megabytes):
    return pltpu.CompilerParams(vmem_limit_bytes=megabytes * 1024 * 1024)


def run_near(count, tok0, w_qkv, w_down, cot):
    outs = [shape(TOKEN, BF16)] * 6 + [shape((TOKENS, HIDDEN), BF16)]
    return pl.pallas_call(
        near_kernel,
        out_shape=outs,
        in_specs=smem(1) + vmem(4),
        out_specs=vmem(len(outs)),
        compiler_params=params(NEAR_MB),
        cost_estimate=pl.CostEstimate(flops=2_500_000_000, bytes_accessed=4_000_000, transcendentals=0),
        name="near",
    )(count, tok0, w_qkv, w_down, cot)


def run_mate(tok1, w_qkv):
    outs = [shape(TOKEN, BF16)] * 4
    return pl.pallas_call(
        mate_kernel,
        out_shape=outs,
        in_specs=vmem(2),
        out_specs=vmem(len(outs)),
        compiler_params=params(NEAR_MB),
        cost_estimate=pl.CostEstimate(flops=5_000_000_000, bytes_accessed=2_000_000, transcendentals=0),
        name="mate",
    )(tok1, w_qkv)


def run_front(core, counts, sectors, w_qkv, w_out, w_up, w_down, cot, near):
    outs = [
        shape(TOKEN, BF16),
        shape((16, 64, 640), BF16),
        shape((16, 64, 640), BF16),
        shape(TOKEN, F32),
        shape(PAIR, BF16),
        shape(PAIR, BF16),
        shape(PAIR, BF16),
        shape(PAIR, BF16),
        shape((6, GROUP, KEYS), BF16),
        shape(TOKEN, BF16),
    ]
    return pl.pallas_call(
        front_kernel,
        out_shape=outs,
        in_specs=smem(5) + vmem(8 + len(near)),
        out_specs=vmem(len(outs)),
        scratch_shapes=[
            pltpu.VMEM(TOKEN, BF16),
            pltpu.VMEM((4, TOKENS, 256), BF16),
            pltpu.VMEM((4, TOKENS, 128), BF16),
            pltpu.VMEM((2, TOKENS, 256), BF16),
        ],
        compiler_params=params(FRONT_MB),
        cost_estimate=pl.CostEstimate(flops=5_000_000_000, bytes_accessed=12_000_000, transcendentals=600_000),
        name="front",
    )(core, *counts, *sectors, w_qkv, w_out, w_up, w_down, cot, *near)


def run_back(core, saved):
    outs = [
        shape((16, 64, 384), BF16),
        shape((16, 64, 384), BF16),
        shape((4, TOKENS, 128), BF16),
        shape((4, 4 * TOKENS, 128), BF16),
        shape((4, 4 * TOKENS, 128), BF16),
    ]
    return pl.pallas_call(
        back_kernel,
        out_shape=outs,
        in_specs=smem(1) + vmem(len(saved)),
        out_specs=vmem(len(outs)),
        compiler_params=params(BACK_MB),
        cost_estimate=pl.CostEstimate(flops=6_000_000_000, bytes_accessed=12_000_000, transcendentals=0),
        name="back",
    )(core, *saved)


def run_push(w_qkv, grads):
    outs = [shape((2,) + TOKEN, BF16), shape(TOKEN, BF16), shape(TOKEN, F32)]
    return pl.pallas_call(
        push_kernel,
        out_shape=outs,
        in_specs=vmem(4),
        out_specs=vmem(3),
        compiler_params=params(NEAR_MB),
        cost_estimate=pl.CostEstimate(flops=2_000_000_000, bytes_accessed=4_000_000, transcendentals=0),
        name="push",
    )(w_qkv, *grads)


def run_join(*halves):
    return pl.pallas_call(
        join_kernel,
        out_shape=shape((16, 64, 1024), BF16),
        in_specs=vmem(4),
        out_specs=vmem(1)[0],
        compiler_params=params(NEAR_MB),
        cost_estimate=pl.CostEstimate(flops=1_000_000, bytes_accessed=6_000_000, transcendentals=0),
        name="join",
    )(*halves)


def run_final(whole):
    outs = [shape((8, 1536), F32), shape((8, 512), F32), shape((8, 1024), F32), shape((16, 512), F32)]
    return pl.pallas_call(
        final_kernel,
        out_shape=outs,
        in_specs=vmem(1),
        out_specs=vmem(4),
        cost_estimate=pl.CostEstimate(flops=1_000_000, bytes_accessed=200_000, transcendentals=0),
        name="final",
    )(whole)


def sum_sources(values):
    return jnp.sum(values.astype(F32), axis=0).astype(BF16)


def swap(values):
    return lax.ppermute(values, "lon", CORE)


def local(tokens, ocean_count, w_qkv, w_out, w_up, w_down, cotangent):
    flat = tokens.reshape(TOKEN)
    cot = cotangent.reshape(TOKEN)
    tok2 = lax.ppermute(flat, "lon", X_LO)
    count2 = lax.ppermute(ocean_count, "lon", X_LO)
    tok1 = swap(flat)
    count1 = swap(ocean_count)
    core = (lax.axis_index("lon") % 2).reshape(1)
    near = run_near(ocean_count, flat, w_qkv, w_down, cot)
    own_kv, query, inv_q, grad_active = near[:4], near[4], near[5], near[6]
    mate_kv = run_mate(tok1, w_qkv)
    tok3 = swap(tok2)
    count3 = swap(count2)
    front = run_front(
        core,
        (ocean_count, count1, count2, count3),
        (flat, tok2, tok3),
        w_qkv,
        w_out,
        w_up,
        w_down,
        cot,
        (query, own_kv[1], own_kv[2], mate_kv[1], mate_kv[2], grad_active),
    )
    block_out, keep1, send1, grad_middle = front[:4]
    recv1 = swap(send1)
    saved = [query, inv_q] + list(own_kv) + list(mate_kv) + list(front[4:])
    keep2, send2, *grads = run_back(core, saved)
    recv2 = swap(send2)
    for_core, for_x, grad_own = run_push(w_qkv, grads)
    joined = run_join(keep1, recv1, keep2, recv2)
    plane = sum_sources(
        lax.all_to_all(joined, ("lat", "lon"), 0, 0, axis_index_groups=PLANE_GROUPS, tiled=True)
    )
    from_core = swap(for_core).astype(F32)
    for_x = (for_x.astype(F32) + from_core[1]).astype(BF16)
    plane, for_x = lax.optimization_barrier((plane, for_x))
    column = sum_sources(
        lax.all_to_all(plane.reshape(8, 8, 1024), "lat", 0, 0, axis_index_groups=Z_GROUPS, tiled=True)
    )
    grad_normed = grad_own + from_core[0] + lax.ppermute(for_x, "lon", X_LO).astype(F32)
    normed, inverse = layer_norm(flat.astype(F32))
    grad_tokens = (grad_middle + layer_norm_back(normed, inverse, grad_normed)).astype(BF16)
    whole = lax.all_gather(column, "lon", axis=0, tiled=True)
    return (block_out.reshape(tokens.shape), grad_tokens.reshape(tokens.shape), *run_final(whole))


def solution(mesh):
    in_specs = (P("lat", "lon", None), P("lat", "lon"), P(), P(), P(), P(), P("lat", "lon", None))
    out_specs = (
        P("lat", "lon", None),
        P("lat", "lon", None),
        P("lat", None),
        P("lat", None),
        P("lat", None),
        P("lat", None),
    )
    return jax.shard_map(local, mesh=mesh, in_specs=in_specs, out_specs=out_specs, check_vma=False)
```

```python
import math

import jax
import jax.numpy as jnp
from jax import lax
from jax.experimental import pallas as pl
from jax.experimental.pallas import tpu as pltpu
from jax.sharding import PartitionSpec as P

F32 = jnp.float32
BF16 = jnp.bfloat16
HEAD_DIM = 64
SOFTMAX_SCALE = 8.0
WIDTH = 512
HIDDEN = 1024
ROWS_DEV = 3
SECTOR = 64
TOKENS = ROWS_DEV * SECTOR
KEYS = 4 * SECTOR
GROUP = 256
GELU_A = math.sqrt(2.0 / math.pi)
GELU_B = 0.044715
NEAR_MB = 20
FRONT_MB = 28
BACK_MB = 28


def lat_index(z, y, x_hi):
    return (z * 4 + y) * 2 + x_hi


CORE = [(0, 1), (1, 0), (2, 3), (3, 2)]
X_LO = [(0, 2), (2, 0), (1, 3), (3, 1)]
DIAGONAL = [(0, 3), (3, 0), (1, 2), (2, 1)]
Z_GROUPS = [[lat_index(z, y, x) for z in range(8)] for y in range(4) for x in range(2)]
PLANE_GROUPS = [
    [lat_index(z, y, x_hi) * 4 + x_lo * 2 + core for y in range(4) for x_hi in range(2) for x_lo in range(2)]
    for z in range(8)
    for core in range(2)
]


def mm(left, right):
    return lax.dot_general(left, right, (((1,), (0,)), ((), ())), preferred_element_type=F32)


def mm_nt(left, right):
    return lax.dot_general(left, right, (((1,), (1,)), ((), ())), preferred_element_type=F32)


def mm_tn(left, right):
    return lax.dot_general(left, right, (((0,), (0,)), ((), ())), preferred_element_type=F32)


def mean_last(values):
    return jnp.sum(values, axis=-1, keepdims=True) * (1.0 / values.shape[-1])


def layer_norm(values):
    centered = values - mean_last(values)
    inverse = lax.rsqrt(mean_last(centered * centered) + 1e-05)
    return centered * inverse, inverse


def layer_norm_back(normed, inverse, grad):
    return inverse * (grad - mean_last(grad) - normed * mean_last(grad * normed))


def head_blocks():
    same = lax.broadcasted_iota(jnp.int32, (GROUP, GROUP), 0) // HEAD_DIM == (
        lax.broadcasted_iota(jnp.int32, (GROUP, GROUP), 1) // HEAD_DIM
    )
    return jnp.where(same, 1.0, 0.0).astype(BF16)


def head_mean(values, blocks):
    parts = [
        mm(values[:, at : at + GROUP].astype(BF16), blocks) for at in range(0, values.shape[1], GROUP)
    ]
    return (parts[0] if len(parts) == 1 else jnp.concatenate(parts, axis=1)) * (1.0 / HEAD_DIM)


def head_masks(dtype):
    lane = lax.broadcasted_iota(jnp.int32, (1, GROUP), 1) // HEAD_DIM
    return [jnp.where(lane == head, 1.0, 0.0).astype(dtype) for head in range(4)]


def stack_heads(values, masks):
    return jnp.concatenate([values * mask for mask in masks], axis=0)


def unstack_heads(values, masks):
    return sum(values[head * SECTOR : (head + 1) * SECTOR] * masks[head] for head in range(4))


def store_pieces(out_ref, x_lo, column, product):
    width = product.shape[1]
    split = product.reshape(8, 8, 8, width)
    for place in range(8):
        piece = jnp.concatenate([split[z, place] for z in range(8)], axis=0)
        out_ref[place * 2 + x_lo, :, column : column + width] = piece.astype(BF16)


def rows_of(row, width=SECTOR):
    return slice(row * width, (row + 1) * width)


def key_value(tok_ref, w_qkv_ref, blocks, slot, slots, normed_ref, key_ref, value_ref, inv_k_ref):
    normed = layer_norm(tok_ref[...].astype(F32))[0].astype(BF16)
    key_raw = mm(normed, w_qkv_ref[:, WIDTH : 2 * WIDTH])
    inv_k = lax.rsqrt(head_mean(key_raw * key_raw, blocks) + 1e-06)
    key_b = (key_raw * inv_k).astype(BF16)
    inv_kb = inv_k.astype(BF16)
    value_b = mm(normed, w_qkv_ref[:, 2 * WIDTH :]).astype(BF16)
    for row in range(ROWS_DEV):
        at = (row * slots + slot) * SECTOR
        for ref, val in (
            (normed_ref, normed),
            (key_ref, key_b),
            (inv_k_ref, inv_kb),
            (value_ref, value_b),
        ):
            ref[at : at + SECTOR, :] = val[rows_of(row)]
    return normed


def own_mask(count_ref):
    place = lax.broadcasted_iota(jnp.int32, (SECTOR, 1), 0)
    return jnp.concatenate(
        [jnp.where(place < count_ref[row, 0], 1.0, 0.0) for row in range(ROWS_DEV)], axis=0
    )


def near_kernel(
    tok0_ref,
    w_qkv_ref,
    normed_ref,
    key_ref,
    value_ref,
    inv_k_ref,
    query_ref,
    inv_q_ref,
):
    blocks = head_blocks()
    normed = key_value(tok0_ref, w_qkv_ref, blocks, 0, 1, normed_ref, key_ref, value_ref, inv_k_ref)
    query_raw = mm(normed, w_qkv_ref[:, :WIDTH])
    inv_q = lax.rsqrt(head_mean(query_raw * query_raw, blocks) + 1e-06)
    inv_q_ref[...] = inv_q.astype(BF16)
    query_ref[...] = (query_raw * inv_q).astype(BF16)


def mate_kernel(
    count_ref,
    tok1_ref,
    w_qkv_ref,
    w_down_ref,
    cot_ref,
    normed_ref,
    key_ref,
    value_ref,
    inv_k_ref,
    grad_active_ref,
):
    branch = (own_mask(count_ref) * cot_ref[...].astype(F32)).astype(BF16)
    grad_active_ref[...] = mm_nt(branch, w_down_ref[...]).astype(BF16)
    key_value(tok1_ref, w_qkv_ref, head_blocks(), 0, 1, normed_ref, key_ref, value_ref, inv_k_ref)


def row_join(row, lanes, own_ref, mate_ref, far_ref):
    own = rows_of(row)
    return jnp.concatenate(
        [own_ref[own, lanes], mate_ref[own, lanes], far_ref[rows_of(row, 2 * SECTOR), lanes]], axis=0
    )


def front_kernel(
    core_ref,
    count_ref,
    count1_ref,
    count2_ref,
    count3_ref,
    tok0_ref,
    tok2_ref,
    tok3_ref,
    w_qkv_ref,
    w_out_ref,
    w_up_ref,
    w_down_ref,
    cot_ref,
    query_ref,
    own_key_ref,
    own_value_ref,
    mate_key_ref,
    mate_value_ref,
    grad_active_ref,
    block_out_ref,
    keep_ref,
    send_ref,
    grad_middle_ref,
    normed_ref,
    key_ref,
    value_ref,
    inv_k_ref,
    probs_ref,
    grad_att_ref,
    att_ref,
    lift_ref,
    attn_ref,
    branch_ref,
):
    blocks = head_blocks()
    masks_b = head_masks(BF16)
    masks_f = head_masks(F32)
    core = core_ref[0]
    key_value(tok2_ref, w_qkv_ref, blocks, 0, 2, normed_ref, key_ref, value_ref, inv_k_ref)
    key_value(tok3_ref, w_qkv_ref, blocks, 1, 2, normed_ref, key_ref, value_ref, inv_k_ref)

    key_place = lax.broadcasted_iota(jnp.int32, (1, KEYS), 1)
    for row in range(ROWS_DEV):
        limit = jnp.zeros((1, KEYS), jnp.int32)
        for sector, ref in enumerate((count_ref, count1_ref, count2_ref, count3_ref)):
            limit = jnp.where(key_place // SECTOR == sector, ref[row, 0], limit)
        key_mask = jnp.where(key_place % SECTOR < limit, 1.0, 0.0)
        for group in range(2):
            lanes = slice(group * GROUP, (group + 1) * GROUP)
            stacked = stack_heads(query_ref[rows_of(row), lanes], masks_b)
            keys = row_join(row, lanes, own_key_ref, mate_key_ref, key_ref)
            values = row_join(row, lanes, own_value_ref, mate_value_ref, value_ref)
            scores = mm_nt(stacked, keys)
            expscore = jnp.exp(scores * (SOFTMAX_SCALE / HEAD_DIM) - SOFTMAX_SCALE) * key_mask
            total = jnp.sum(expscore, axis=1, keepdims=True)
            probs = (expscore * (1.0 / total)).astype(BF16)
            probs_ref[row * 2 + group] = probs
            att_ref[rows_of(row), lanes] = unstack_heads(mm(probs, values), masks_f).astype(BF16)

    mask = own_mask(count_ref)
    attended = att_ref[...]
    middle = tok0_ref[...].astype(F32) + mask * mm(attended, w_out_ref[...])
    normed_two, inverse = layer_norm(middle)
    normed_two_b = normed_two.astype(BF16)
    lifted = mm(normed_two_b, w_up_ref[...])
    square = lifted * lifted
    bent = jnp.tanh(GELU_A * lifted * (1.0 + GELU_B * square))
    half = 0.5 * (1.0 + bent)
    active = (lifted * half).astype(BF16)
    slope = half + 0.5 * lifted * (1.0 - bent * bent) * (GELU_A * (1.0 + 3.0 * GELU_B * square))
    block_out_ref[...] = (middle + mask * mm(active, w_down_ref[...])).astype(BF16)
    upstream = cot_ref[...].astype(F32)
    branch = (mask * upstream).astype(BF16)
    grad_lifted = (slope * grad_active_ref[...].astype(F32)).astype(BF16)
    grad_normed = mm_nt(grad_lifted, w_up_ref[...])
    grad_middle = upstream + layer_norm_back(normed_two, inverse, grad_normed)
    grad_middle_ref[...] = grad_middle
    grad_attn = (mask * grad_middle).astype(BF16)
    grad_att_ref[...] = mm_nt(grad_attn, w_out_ref[...]).astype(BF16)

    for part in range(4):
        lift_ref[part] = grad_lifted[:, part * 256 : (part + 1) * 256]
        attn_ref[part] = grad_attn[:, part * 128 : (part + 1) * 128]
    for part in range(2):
        branch_ref[part] = branch[:, part * 256 : (part + 1) * 256]
    attended_t, normed_two_t, active_t = attended.T, normed_two_b.T, active.T
    for out_ref, half_index in ((keep_ref, core), (send_ref, 1 - core)):
        pair = jnp.concatenate([attn_ref[half_index], attn_ref[half_index + 2]], axis=1)
        term_out = mm(attended_t, pair)
        for x_lo in range(2):
            store_pieces(out_ref, x_lo, 0, term_out[:, x_lo * 128 : (x_lo + 1) * 128])
            store_pieces(out_ref, x_lo, 128, mm(normed_two_t, lift_ref[half_index + 2 * x_lo]))
        term_down = mm(active_t, branch_ref[half_index]).reshape(64, 2, 8, 256)
        for x_lo in range(2):
            store_pieces(out_ref, x_lo, 384, term_down[:, x_lo].reshape(512, 256))


def norm_back(normed_b, inverse_b, grad, blocks):
    normed = normed_b.astype(F32)
    shift = head_mean(normed * grad, blocks)
    return (inverse_b.astype(F32) * (grad - normed * shift)).astype(BF16)


def back_kernel(
    core_ref,
    query_ref,
    inv_q_ref,
    own_normed_ref,
    own_key_ref,
    own_value_ref,
    own_inv_k_ref,
    mate_normed_ref,
    mate_key_ref,
    mate_value_ref,
    mate_inv_k_ref,
    normed_ref,
    key_ref,
    value_ref,
    inv_k_ref,
    probs_ref,
    grad_att_ref,
    keep_ref,
    send_ref,
    gq_ref,
    gk_ref,
    gv_ref,
):
    blocks = head_blocks()
    masks_b = head_masks(BF16)
    masks_f = head_masks(F32)
    core = core_ref[0]
    for row in range(ROWS_DEV):
        own = rows_of(row)
        mate = slice(own.start + TOKENS, own.stop + TOKENS)
        far = rows_of(row, 2 * SECTOR)
        far = slice(far.start + 2 * TOKENS, far.stop + 2 * TOKENS)
        for group in range(2):
            lanes = slice(group * GROUP, (group + 1) * GROUP)
            keys = row_join(row, lanes, own_key_ref, mate_key_ref, key_ref)
            values = row_join(row, lanes, own_value_ref, mate_value_ref, value_ref)
            inv_k = row_join(row, lanes, own_inv_k_ref, mate_inv_k_ref, inv_k_ref)
            stacked_q = stack_heads(query_ref[own, lanes], masks_b)
            stacked_g = stack_heads(grad_att_ref[own, lanes], masks_b)
            probs_b = probs_ref[row * 2 + group]
            probs = probs_b.astype(F32)
            grad_probs = mm_nt(stacked_g, values)
            delta = jnp.sum(probs * grad_probs, axis=1, keepdims=True)
            grad_scores = (probs * (grad_probs - delta) * (SOFTMAX_SCALE / HEAD_DIM)).astype(BF16)
            grad_q = unstack_heads(mm(grad_scores, keys), masks_f)
            grad_k = mm_tn(grad_scores, stacked_q)
            grad_v = mm_tn(probs_b, stacked_g).astype(BF16)
            grad_q = norm_back(query_ref[own, lanes], inv_q_ref[own, lanes], grad_q, blocks)
            grad_k = norm_back(keys, inv_k, grad_k, blocks)
            for part in range(2):
                at = slice(part * 128, (part + 1) * 128)
                gq_ref[group * 2 + part, own, :] = grad_q[:, at]
                for ref, grad in ((gk_ref, grad_k), (gv_ref, grad_v)):
                    ref[group * 2 + part, own, :] = grad[:SECTOR, at]
                    ref[group * 2 + part, mate, :] = grad[SECTOR : 2 * SECTOR, at]
                    ref[group * 2 + part, far, :] = grad[2 * SECTOR :, at]

    normed_all = jnp.concatenate([own_normed_ref[...], mate_normed_ref[...], normed_ref[...]], axis=0)
    own_normed_t, normed_all_t = own_normed_ref[...].T, normed_all.T
    for out_ref, half_index in ((keep_ref, core), (send_ref, 1 - core)):
        pair = jnp.concatenate([gq_ref[half_index], gq_ref[half_index + 2]], axis=1)
        term_q = mm(own_normed_t, pair)
        for x_lo in range(2):
            store_pieces(out_ref, x_lo, 0, term_q[:, x_lo * 128 : (x_lo + 1) * 128])
            pair = jnp.concatenate([gk_ref[half_index + 2 * x_lo], gv_ref[half_index + 2 * x_lo]], axis=1)
            store_pieces(out_ref, x_lo, 128, mm(normed_all_t, pair))


def push_kernel(w_qkv_ref, gq_ref, gk_ref, gv_ref, for_core_ref, for_x_ref, own_ref):
    grad_q = jnp.concatenate([gq_ref[part] for part in range(4)], axis=1)

    def grad_normed(rows):
        grads = [ref[part, rows, :] for ref in (gk_ref, gv_ref) for part in range(4)]
        return mm_nt(jnp.concatenate(grads, axis=1), w_qkv_ref[:, WIDTH:])

    for_core_ref[0] = grad_normed(slice(TOKENS, 2 * TOKENS)).astype(BF16)
    far = grad_normed(slice(2 * TOKENS, 4 * TOKENS)).astype(BF16)
    for row in range(ROWS_DEV):
        at = row * 2 * SECTOR
        for_x_ref[rows_of(row), :] = far[at : at + SECTOR]
        for_core_ref[1, rows_of(row), :] = far[at + SECTOR : at + 2 * SECTOR]
    own_ref[...] = grad_normed(slice(0, TOKENS)) + mm_nt(grad_q, w_qkv_ref[:, :WIDTH])


def join_kernel(keep1_ref, recv1_ref, keep2_ref, recv2_ref, after_ref, out_ref):
    del after_ref
    for piece in range(16):
        out_ref[piece, :, :384] = (keep2_ref[piece].astype(F32) + recv2_ref[piece].astype(F32)).astype(BF16)
        out_ref[piece, :, 384:] = (keep1_ref[piece].astype(F32) + recv1_ref[piece].astype(F32)).astype(BF16)


def add_x_kernel(for_x_ref, recv_core_ref, out_ref):
    out_ref[...] = (for_x_ref[...].astype(F32) + recv_core_ref[1].astype(F32)).astype(BF16)


def sum_kernel(parts_ref, out_ref):
    total = parts_ref[0].astype(F32)
    for part in range(1, parts_ref.shape[0]):
        total = total + parts_ref[part].astype(F32)
    out_ref[...] = total.astype(BF16)


def finish_kernel(tok_ref, own_ref, recv_core_ref, from_x_ref, middle_ref, out_ref):
    grad = own_ref[...] + recv_core_ref[0].astype(F32) + from_x_ref[...].astype(F32)
    normed, inverse = layer_norm(tok_ref[...].astype(F32))
    out_ref[...] = (middle_ref[...] + layer_norm_back(normed, inverse, grad)).astype(BF16)


def final_kernel(lon_ref, own_ref, core_ref, x_ref, diagonal_ref, qkv_ref, out_ref, up_ref, down_ref):
    lon = lon_ref[0]
    scale = 1.0 / math.sqrt(64 * 4 * TOKENS)
    held = [ref[...].astype(F32) * scale for ref in (own_ref, core_ref, x_ref, diagonal_ref)]
    for quarter in range(4):
        part = held[3]
        for distance in range(3):
            part = jnp.where(lon == (quarter ^ distance), held[distance], part)
        at = slice(quarter * 128, (quarter + 1) * 128)
        for matrix in range(3):
            low = matrix * WIDTH + quarter * 128
            qkv_ref[:, low : low + 128] = part[:, matrix * 128 : (matrix + 1) * 128]
        out_ref[:, at] = part[:, 384:512]
        up_ref[:, quarter * 256 : (quarter + 1) * 256] = part[:, 512:768]
        side = (quarter % 2) * 256
        down_ref[(quarter // 2) * 8 : (quarter // 2) * 8 + 8, side : side + 256] = part[:, 768:]


def vmem(count):
    return [pl.BlockSpec(memory_space=pltpu.VMEM)] * count


def smem(count):
    return [pl.BlockSpec(memory_space=pltpu.SMEM)] * count


def shape(dims, dtype):
    return jax.ShapeDtypeStruct(dims, dtype)


TOKEN = (TOKENS, WIDTH)
PAIR = (2 * TOKENS, WIDTH)


def params(megabytes):
    return pltpu.CompilerParams(vmem_limit_bytes=megabytes * 1024 * 1024)


def run_near(tok0, w_qkv):
    outs = [shape(TOKEN, BF16)] * 6
    return pl.pallas_call(
        near_kernel,
        out_shape=outs,
        in_specs=vmem(2),
        out_specs=vmem(len(outs)),
        compiler_params=params(NEAR_MB),
        cost_estimate=pl.CostEstimate(flops=2_500_000_000, bytes_accessed=4_000_000, transcendentals=0),
        name="near",
    )(tok0, w_qkv)


def run_mate(count, tok1, w_qkv, w_down, cot):
    outs = [shape(TOKEN, BF16)] * 4 + [shape((TOKENS, HIDDEN), BF16)]
    return pl.pallas_call(
        mate_kernel,
        out_shape=outs,
        in_specs=smem(1) + vmem(4),
        out_specs=vmem(len(outs)),
        compiler_params=params(NEAR_MB),
        cost_estimate=pl.CostEstimate(flops=5_000_000_000, bytes_accessed=2_000_000, transcendentals=0),
        name="mate",
    )(count, tok1, w_qkv, w_down, cot)


def run_front(core, counts, sectors, w_qkv, w_out, w_up, w_down, cot, near):
    outs = [
        shape(TOKEN, BF16),
        shape((16, 64, 640), BF16),
        shape((16, 64, 640), BF16),
        shape(TOKEN, F32),
        shape(PAIR, BF16),
        shape(PAIR, BF16),
        shape(PAIR, BF16),
        shape(PAIR, BF16),
        shape((6, GROUP, KEYS), BF16),
        shape(TOKEN, BF16),
    ]
    return pl.pallas_call(
        front_kernel,
        out_shape=outs,
        in_specs=smem(5) + vmem(8 + len(near)),
        out_specs=vmem(len(outs)),
        scratch_shapes=[
            pltpu.VMEM(TOKEN, BF16),
            pltpu.VMEM((4, TOKENS, 256), BF16),
            pltpu.VMEM((4, TOKENS, 128), BF16),
            pltpu.VMEM((2, TOKENS, 256), BF16),
        ],
        compiler_params=params(FRONT_MB),
        cost_estimate=pl.CostEstimate(flops=5_000_000_000, bytes_accessed=12_000_000, transcendentals=600_000),
        name="front",
    )(core, *counts, *sectors, w_qkv, w_out, w_up, w_down, cot, *near)


def run_back(core, saved):
    outs = [
        shape((16, 64, 384), BF16),
        shape((16, 64, 384), BF16),
        shape((4, TOKENS, 128), BF16),
        shape((4, 4 * TOKENS, 128), BF16),
        shape((4, 4 * TOKENS, 128), BF16),
    ]
    return pl.pallas_call(
        back_kernel,
        out_shape=outs,
        in_specs=smem(1) + vmem(len(saved)),
        out_specs=vmem(len(outs)),
        compiler_params=params(BACK_MB),
        cost_estimate=pl.CostEstimate(flops=6_000_000_000, bytes_accessed=12_000_000, transcendentals=0),
        name="back",
    )(core, *saved)


def run_push(w_qkv, grads):
    outs = [shape((2,) + TOKEN, BF16), shape(TOKEN, BF16), shape(TOKEN, F32)]
    return pl.pallas_call(
        push_kernel,
        out_shape=outs,
        in_specs=vmem(4),
        out_specs=vmem(3),
        compiler_params=params(NEAR_MB),
        cost_estimate=pl.CostEstimate(flops=2_000_000_000, bytes_accessed=4_000_000, transcendentals=0),
        name="push",
    )(w_qkv, *grads)


def small_call(kernel, outs, scalars, arrays, name):
    return pl.pallas_call(
        kernel,
        out_shape=outs,
        in_specs=smem(len(scalars)) + vmem(len(arrays)),
        out_specs=vmem(len(outs)),
        compiler_params=params(NEAR_MB),
        cost_estimate=pl.CostEstimate(flops=1_000_000, bytes_accessed=4_000_000, transcendentals=0),
        name=name,
    )(*scalars, *arrays)


def run_join(keep1, recv1, keep2, recv2, after):
    return pl.pallas_call(
        join_kernel,
        out_shape=shape((16, 64, 1024), BF16),
        in_specs=vmem(4) + [pl.BlockSpec(memory_space=pl.ANY)],
        out_specs=vmem(1)[0],
        compiler_params=params(NEAR_MB),
        cost_estimate=pl.CostEstimate(flops=1_000_000, bytes_accessed=4_000_000, transcendentals=0),
        name="join",
    )(keep1, recv1, keep2, recv2, after)


def run_add_x(*parts):
    return small_call(add_x_kernel, [shape(TOKEN, BF16)], [], parts, "add_x")[0]


def run_sum(parts):
    return small_call(sum_kernel, [shape((64, 1024), BF16)], [], [parts], "plane_sum")[0]


def run_finish(*parts):
    return small_call(finish_kernel, [shape(TOKEN, BF16)], [], parts, "finish")[0]


def run_final(lon, parts):
    outs = [shape((8, 1536), F32), shape((8, 512), F32), shape((8, 1024), F32), shape((16, 512), F32)]
    return small_call(final_kernel, outs, [lon], parts, "final")


def sum_sources(values):
    return jnp.sum(values.astype(F32), axis=0).astype(BF16)


def swap(values):
    return lax.ppermute(values, "lon", CORE)


def local(tokens, ocean_count, w_qkv, w_out, w_up, w_down, cotangent):
    flat = tokens.reshape(TOKEN)
    cot = cotangent.reshape(TOKEN)
    tok2 = lax.ppermute(flat, "lon", X_LO)
    count2 = lax.ppermute(ocean_count, "lon", X_LO)
    tok1 = swap(flat)
    count1 = swap(ocean_count)
    lon = lax.axis_index("lon")
    core = (lon % 2).reshape(1)
    *own_kv, query, inv_q = run_near(flat, w_qkv)
    *mate_kv, grad_active = run_mate(ocean_count, tok1, w_qkv, w_down, cot)
    tok3 = swap(tok2)
    count3 = swap(count2)
    front = run_front(
        core,
        (ocean_count, count1, count2, count3),
        (flat, tok2, tok3),
        w_qkv,
        w_out,
        w_up,
        w_down,
        cot,
        (query, own_kv[1], own_kv[2], mate_kv[1], mate_kv[2], grad_active),
    )
    block_out, keep1, send1, grad_middle = front[:4]
    recv1 = swap(send1)
    saved = [query, inv_q] + list(own_kv) + list(mate_kv) + list(front[4:])
    keep2, send2, *grads = run_back(core, saved)
    recv2 = swap(send2)
    for_core, for_x, grad_own = run_push(w_qkv, grads)
    recv_core = swap(for_core)
    joined = run_join(keep1, recv1, keep2, recv2, recv_core)
    plane = lax.all_to_all(joined, ("lat", "lon"), 0, 0, axis_index_groups=PLANE_GROUPS, tiled=True)
    plane, for_x, recv_core = lax.optimization_barrier((run_sum(plane), for_x, recv_core))
    from_x = lax.ppermute(run_add_x(for_x, recv_core), "lon", X_LO)
    column = sum_sources(
        lax.all_to_all(plane.reshape(8, 8, 1024), "lat", 0, 0, axis_index_groups=Z_GROUPS, tiled=True)
    )
    gathered = [column] + [lax.ppermute(column, "lon", table) for table in (CORE, X_LO, DIAGONAL)]
    grad_tokens = run_finish(flat, grad_own, recv_core, from_x, grad_middle)
    weights = run_final(lon.reshape(1), gathered)
    return (block_out.reshape(tokens.shape), grad_tokens.reshape(tokens.shape), *weights)


def solution(mesh):
    in_specs = (P("lat", "lon", None), P("lat", "lon"), P(), P(), P(), P(), P("lat", "lon", None))
    out_specs = (
        P("lat", "lon", None),
        P("lat", "lon", None),
        P("lat", None),
        P("lat", None),
        P("lat", None),
        P("lat", None),
    )
    return jax.shard_map(local, mesh=mesh, in_specs=in_specs, out_specs=out_specs, check_vma=False)
```

```python
import math

import jax
import jax.numpy as jnp
from jax import lax
from jax.experimental import pallas as pl
from jax.experimental.pallas import tpu as pltpu
from jax.sharding import PartitionSpec as P

F32 = jnp.float32
BF16 = jnp.bfloat16
HEAD_DIM = 64
SOFTMAX_SCALE = 8.0
WIDTH = 512
HIDDEN = 1024
ROWS_DEV = 3
SECTOR = 64
TOKENS = ROWS_DEV * SECTOR
KEYS = 4 * SECTOR
GROUP = 256
GELU_A = math.sqrt(2.0 / math.pi)
GELU_B = 0.044715
NEAR_MB = 20
FRONT_MB = 28
BACK_MB = 28


def lat_index(z, y, x_hi):
    return (z * 4 + y) * 2 + x_hi


CORE = [(0, 1), (1, 0), (2, 3), (3, 2)]
X_LO = [(0, 2), (2, 0), (1, 3), (3, 1)]
DIAGONAL = [(0, 3), (3, 0), (1, 2), (2, 1)]
Z_ORDER = (0, 7, 1, 6, 2, 5, 3, 4)
Z_GROUPS = [[lat_index(z, y, x) for z in Z_ORDER] for y in range(4) for x in range(2)]
PLANE_GROUPS = [
    [
        lat_index(z, y, x_hi) * 4 + x_lo * 2 + core
        for y in reversed(range(4))
        for x_hi in reversed(range(2))
        for x_lo in reversed(range(2))
    ]
    for z in range(8)
    for core in range(2)
]


def mm(left, right):
    return lax.dot_general(left, right, (((1,), (0,)), ((), ())), preferred_element_type=F32)


def mm_nt(left, right):
    return lax.dot_general(left, right, (((1,), (1,)), ((), ())), preferred_element_type=F32)


def mm_tn(left, right):
    return lax.dot_general(left, right, (((0,), (0,)), ((), ())), preferred_element_type=F32)


def mean_last(values):
    return jnp.sum(values, axis=-1, keepdims=True) * (1.0 / values.shape[-1])


def layer_norm(values):
    centered = values - mean_last(values)
    inverse = lax.rsqrt(mean_last(centered * centered) + 1e-05)
    return centered * inverse, inverse


def layer_norm_back(normed, inverse, grad):
    return inverse * (grad - mean_last(grad) - normed * mean_last(grad * normed))


def head_blocks():
    same = lax.broadcasted_iota(jnp.int32, (GROUP, GROUP), 0) // HEAD_DIM == (
        lax.broadcasted_iota(jnp.int32, (GROUP, GROUP), 1) // HEAD_DIM
    )
    return jnp.where(same, 1.0, 0.0).astype(BF16)


def head_mean(values, blocks):
    parts = [
        mm(values[:, at : at + GROUP].astype(BF16), blocks) for at in range(0, values.shape[1], GROUP)
    ]
    return (parts[0] if len(parts) == 1 else jnp.concatenate(parts, axis=1)) * (1.0 / HEAD_DIM)


def head_masks(dtype):
    lane = lax.broadcasted_iota(jnp.int32, (1, GROUP), 1) // HEAD_DIM
    return [jnp.where(lane == head, 1.0, 0.0).astype(dtype) for head in range(4)]


def stack_heads(values, masks):
    return jnp.concatenate([values * mask for mask in masks], axis=0)


def unstack_heads(values, masks):
    return sum(values[head * SECTOR : (head + 1) * SECTOR] * masks[head] for head in range(4))


def store_pieces(out_ref, x_lo, column, product):
    width = product.shape[1]
    split = product.reshape(8, 8, 8, width)
    for place in range(8):
        piece = jnp.concatenate([split[z, place] for z in Z_ORDER], axis=0)
        out_ref[15 - place * 2 - x_lo, :, column : column + width] = piece.astype(BF16)


def rows_of(row, width=SECTOR):
    return slice(row * width, (row + 1) * width)


def key_value(tok_refs, w_qkv_ref, blocks, *out_refs):
    tokens = jnp.concatenate([ref[...] for ref in tok_refs], axis=0).astype(F32)
    normed = layer_norm(tokens)[0].astype(BF16)
    key_raw = mm(normed, w_qkv_ref[:, WIDTH : 2 * WIDTH])
    value = mm(normed, w_qkv_ref[:, 2 * WIDTH :]).astype(BF16)
    inv_k = lax.rsqrt(head_mean(key_raw * key_raw, blocks) + 1e-06)
    made = (normed, (key_raw * inv_k).astype(BF16), value, inv_k.astype(BF16))
    for at, ref in enumerate(out_refs):
        first = at // 4 * TOKENS
        ref[...] = made[at % 4][first : first + TOKENS]
    return normed


def own_mask(count_ref):
    place = lax.broadcasted_iota(jnp.int32, (SECTOR, 1), 0)
    return jnp.concatenate(
        [jnp.where(place < count_ref[0, row], 1.0, 0.0) for row in range(ROWS_DEV)], axis=0
    )


def near_kernel(tok0_ref, w_qkv_ref, query_ref, inv_q_ref, *own_refs):
    blocks = head_blocks()
    normed = key_value([tok0_ref], w_qkv_ref, blocks, *own_refs)
    query_raw = mm(normed, w_qkv_ref[:, :WIDTH])
    inv_q = lax.rsqrt(head_mean(query_raw * query_raw, blocks) + 1e-06)
    inv_q_ref[...] = inv_q.astype(BF16)
    query_ref[...] = (query_raw * inv_q).astype(BF16)


def pair_kernel(count_ref, tok1_ref, tok2_ref, w_qkv_ref, w_down_ref, cot_ref, grad_active_ref, *refs):
    blocks = head_blocks()
    branch = (own_mask(count_ref) * cot_ref[...].astype(F32)).astype(BF16)
    grad_active_ref[...] = mm_nt(branch, w_down_ref[...]).astype(BF16)
    key_value([tok1_ref, tok2_ref], w_qkv_ref, blocks, *refs)


PLACES = [(row, slice(low, low + GROUP)) for row in range(ROWS_DEV) for low in (0, GROUP)]


def row_join(row, lanes, refs):
    return jnp.concatenate([ref[rows_of(row), lanes] for ref in refs], axis=0)


def front_kernel(
    core_ref,
    count_ref,
    count1_ref,
    count2_ref,
    count3_ref,
    tok0_ref,
    tok3_ref,
    w_qkv_ref,
    w_out_ref,
    w_up_ref,
    w_down_ref,
    cot_ref,
    query_ref,
    own_key_ref,
    own_value_ref,
    mate_key_ref,
    mate_value_ref,
    across_key_ref,
    across_value_ref,
    grad_active_ref,
    block_out_ref,
    keep_ref,
    send_ref,
    grad_middle_ref,
    normed_ref,
    key_ref,
    value_ref,
    inv_k_ref,
    probs_ref,
    grad_att_ref,
    att_ref,
    lift_ref,
    attn_ref,
    branch_ref,
):
    blocks = head_blocks()
    masks_b = head_masks(BF16)
    masks_f = head_masks(F32)
    core = core_ref[0]
    key_value([tok3_ref], w_qkv_ref, blocks, normed_ref, key_ref, value_ref, inv_k_ref)
    key_refs = (own_key_ref, mate_key_ref, across_key_ref, key_ref)
    value_refs = (own_value_ref, mate_value_ref, across_value_ref, value_ref)

    key_place = lax.broadcasted_iota(jnp.int32, (1, KEYS), 1)
    key_masks = []
    for row in range(ROWS_DEV):
        limit = jnp.zeros((1, KEYS), jnp.int32)
        for sector, ref in enumerate((count_ref, count1_ref, count2_ref, count3_ref)):
            limit = jnp.where(key_place // SECTOR == sector, ref[0, row], limit)
        key_masks.append(jnp.where(key_place % SECTOR < limit, 1.0, 0.0))
    scores = [
        mm_nt(stack_heads(query_ref[rows_of(row), lanes], masks_b), row_join(row, lanes, key_refs))
        for row, lanes in PLACES
    ]
    for at, (row, lanes) in enumerate(PLACES):
        expscore = jnp.exp(scores[at] * (SOFTMAX_SCALE / HEAD_DIM) - SOFTMAX_SCALE) * key_masks[row]
        total = jnp.sum(expscore, axis=1, keepdims=True)
        probs_ref[at] = (expscore * (1.0 / total)).astype(BF16)
    mixed = [mm(probs_ref[at], row_join(row, lanes, value_refs)) for at, (row, lanes) in enumerate(PLACES)]
    for at, (row, lanes) in enumerate(PLACES):
        att_ref[rows_of(row), lanes] = unstack_heads(mixed[at], masks_f).astype(BF16)

    mask = own_mask(count_ref)
    attended = att_ref[...]
    middle = tok0_ref[...].astype(F32) + mask * mm(attended, w_out_ref[...])
    normed_two, inverse = layer_norm(middle)
    normed_two_b = normed_two.astype(BF16)
    lifted = mm(normed_two_b, w_up_ref[...])
    square = lifted * lifted
    bent = jnp.tanh(GELU_A * lifted * (1.0 + GELU_B * square))
    half = 0.5 * (1.0 + bent)
    active = (lifted * half).astype(BF16)
    slope = half + 0.5 * lifted * (1.0 - bent * bent) * (GELU_A * (1.0 + 3.0 * GELU_B * square))
    branch = (mask * cot_ref[...].astype(F32)).astype(BF16)
    grad_lifted = (slope * grad_active_ref[...].astype(F32)).astype(BF16)
    grad_normed = mm_nt(grad_lifted, w_up_ref[...])
    for part in range(2):
        branch_ref[part] = branch[:, part * 256 : (part + 1) * 256]
    for part in range(4):
        lift_ref[part] = grad_lifted[:, part * 256 : (part + 1) * 256]
    halves = ((keep_ref, core), (send_ref, 1 - core))
    active_t, normed_two_t = active.T, normed_two_b.T
    for out_ref, half_index in halves:
        term_down = mm(active_t, branch_ref[half_index]).reshape(64, 2, 8, 256)
        for x_lo in range(2):
            store_pieces(out_ref, x_lo, 384, term_down[:, x_lo].reshape(512, 256))
    grad_middle = cot_ref[...].astype(F32) + layer_norm_back(normed_two, inverse, grad_normed)
    grad_middle_ref[...] = grad_middle
    grad_attn = (mask * grad_middle).astype(BF16)
    grad_att_ref[...] = mm_nt(grad_attn, w_out_ref[...]).astype(BF16)
    block_out_ref[...] = (middle + mask * mm(active, w_down_ref[...])).astype(BF16)
    for out_ref, half_index in halves:
        for x_lo in range(2):
            store_pieces(out_ref, x_lo, 128, mm(normed_two_t, lift_ref[half_index + 2 * x_lo]))
    for part in range(4):
        attn_ref[part] = grad_attn[:, part * 128 : (part + 1) * 128]
    attended_t = attended.T
    for out_ref, half_index in halves:
        pair = jnp.concatenate([attn_ref[half_index], attn_ref[half_index + 2]], axis=1)
        term_out = mm(attended_t, pair)
        for x_lo in range(2):
            store_pieces(out_ref, x_lo, 0, term_out[:, x_lo * 128 : (x_lo + 1) * 128])


def norm_back(normed_b, inverse_b, grad, blocks):
    normed = normed_b.astype(F32)
    shift = head_mean(normed * grad, blocks)
    return (inverse_b.astype(F32) * (grad - normed * shift)).astype(BF16)


def back_kernel(core_ref, query_ref, inv_q_ref, *refs):
    sectors, (probs_ref, grad_att_ref, keep_ref, send_ref, gq_ref, gk_ref, gv_ref) = refs[:16], refs[16:]
    normed_refs, key_refs, value_refs, inv_k_refs = (sectors[at::4] for at in range(4))
    blocks = head_blocks()
    masks_b = head_masks(BF16)
    masks_f = head_masks(F32)
    core = core_ref[0]
    stacked_q = [stack_heads(query_ref[rows_of(row), lanes], masks_b) for row, lanes in PLACES]
    stacked_g = [stack_heads(grad_att_ref[rows_of(row), lanes], masks_b) for row, lanes in PLACES]
    keys = [row_join(row, lanes, key_refs) for row, lanes in PLACES]
    grad_probs = [
        mm_nt(stacked_g[at], row_join(row, lanes, value_refs)) for at, (row, lanes) in enumerate(PLACES)
    ]
    grad_scores = []
    for at in range(len(PLACES)):
        probs = probs_ref[at].astype(F32)
        delta = jnp.sum(probs * grad_probs[at], axis=1, keepdims=True)
        grad_scores.append((probs * (grad_probs[at] - delta) * (SOFTMAX_SCALE / HEAD_DIM)).astype(BF16))
    grad_v = [mm_tn(probs_ref[at], stacked_g[at]).astype(BF16) for at in range(len(PLACES))]
    grad_k = [mm_tn(grad_scores[at], stacked_q[at]) for at in range(len(PLACES))]
    grad_q = [unstack_heads(mm(grad_scores[at], keys[at]), masks_f) for at in range(len(PLACES))]
    for at, (row, lanes) in enumerate(PLACES):
        own = rows_of(row)
        back_q = norm_back(query_ref[own, lanes], inv_q_ref[own, lanes], grad_q[at], blocks)
        back_k = norm_back(keys[at], row_join(row, lanes, inv_k_refs), grad_k[at], blocks)
        for part in range(2):
            cut = slice(part * 128, (part + 1) * 128)
            quarter = lanes.start // 128 + part
            gq_ref[quarter, own, :] = back_q[:, cut]
            for ref, grad in ((gk_ref, back_k), (gv_ref, grad_v[at])):
                for sector in range(4):
                    rows = slice(sector * TOKENS + own.start, sector * TOKENS + own.stop)
                    ref[quarter, rows, :] = grad[sector * SECTOR : (sector + 1) * SECTOR, cut]

    normed_all = jnp.concatenate([ref[...] for ref in normed_refs], axis=0)
    own_normed_t, normed_all_t = normed_refs[0][...].T, normed_all.T
    for out_ref, half_index in ((keep_ref, core), (send_ref, 1 - core)):
        pair = jnp.concatenate([gq_ref[half_index], gq_ref[half_index + 2]], axis=1)
        term_q = mm(own_normed_t, pair)
        for x_lo in range(2):
            store_pieces(out_ref, x_lo, 0, term_q[:, x_lo * 128 : (x_lo + 1) * 128])
            pair = jnp.concatenate([gk_ref[half_index + 2 * x_lo], gv_ref[half_index + 2 * x_lo]], axis=1)
            store_pieces(out_ref, x_lo, 128, mm(normed_all_t, pair))


def push_kernel(w_qkv_ref, gq_ref, gk_ref, gv_ref, for_core_ref, for_x_ref, own_ref):
    grad_q = jnp.concatenate([gq_ref[part] for part in range(4)], axis=1)
    grad_kv = jnp.concatenate([ref[part] for ref in (gk_ref, gv_ref) for part in range(4)], axis=1)
    grad_normed = mm_nt(grad_kv, w_qkv_ref[:, WIDTH:])
    for_core_ref[0] = grad_normed[TOKENS : 2 * TOKENS].astype(BF16)
    for_x_ref[...] = grad_normed[2 * TOKENS : 3 * TOKENS].astype(BF16)
    for_core_ref[1] = grad_normed[3 * TOKENS :].astype(BF16)
    own_ref[...] = grad_normed[:TOKENS] + mm_nt(grad_q, w_qkv_ref[:, :WIDTH])


def join_kernel(keep1_ref, recv1_ref, keep2_ref, recv2_ref, after_ref, out_ref):
    del after_ref
    for piece in range(16):
        out_ref[piece, :, :384] = (keep2_ref[piece].astype(F32) + recv2_ref[piece].astype(F32)).astype(BF16)
        out_ref[piece, :, 384:] = (keep1_ref[piece].astype(F32) + recv1_ref[piece].astype(F32)).astype(BF16)


def add_x_kernel(for_x_ref, recv_core_ref, out_ref):
    out_ref[...] = (for_x_ref[...].astype(F32) + recv_core_ref[1].astype(F32)).astype(BF16)


def sum_kernel(parts_ref, out_ref):
    total = parts_ref[0].astype(F32)
    for part in range(1, parts_ref.shape[0]):
        total = total + parts_ref[part].astype(F32)
    out_ref[...] = total.astype(BF16)


def finish_kernel(tok_ref, own_ref, recv_core_ref, from_x_ref, middle_ref, out_ref, done_ref):
    done_ref[...] = jnp.zeros((8, 128), F32)
    grad = own_ref[...] + recv_core_ref[0].astype(F32) + from_x_ref[...].astype(F32)
    normed, inverse = layer_norm(tok_ref[...].astype(F32))
    out_ref[...] = (middle_ref[...] + layer_norm_back(normed, inverse, grad)).astype(BF16)


def final_kernel(lon_ref, after_ref, own_ref, core_ref, x_ref, diagonal_ref, qkv_ref, out_ref, up_ref, down_ref):
    del after_ref
    lon = lon_ref[0]
    scale = 1.0 / math.sqrt(64 * 4 * TOKENS)
    held = [ref[...].astype(F32) * scale for ref in (own_ref, core_ref, x_ref, diagonal_ref)]
    for quarter in range(4):
        part = held[3]
        for distance in range(3):
            part = jnp.where(lon == (quarter ^ distance), held[distance], part)
        at = slice(quarter * 128, (quarter + 1) * 128)
        for matrix in range(3):
            low = matrix * WIDTH + quarter * 128
            qkv_ref[:, low : low + 128] = part[:, matrix * 128 : (matrix + 1) * 128]
        out_ref[:, at] = part[:, 384:512]
        up_ref[:, quarter * 256 : (quarter + 1) * 256] = part[:, 512:768]
        side = (quarter % 2) * 256
        down_ref[(quarter // 2) * 8 : (quarter // 2) * 8 + 8, side : side + 256] = part[:, 768:]


def vmem(count):
    return [pl.BlockSpec(memory_space=pltpu.VMEM)] * count


def smem(count):
    return [pl.BlockSpec(memory_space=pltpu.SMEM)] * count


def shape(dims, dtype):
    return jax.ShapeDtypeStruct(dims, dtype)


TOKEN = (TOKENS, WIDTH)


def params(megabytes):
    return pltpu.CompilerParams(vmem_limit_bytes=megabytes * 1024 * 1024)


def run_near(tok0, w_qkv):
    outs = [shape(TOKEN, BF16)] * 6
    return pl.pallas_call(
        near_kernel,
        out_shape=outs,
        in_specs=vmem(2),
        out_specs=vmem(len(outs)),
        compiler_params=params(NEAR_MB),
        cost_estimate=pl.CostEstimate(flops=2_500_000_000, bytes_accessed=4_000_000, transcendentals=0),
        name="near",
    )(tok0, w_qkv)


def run_pair(count, tok1, tok2, w_qkv, w_down, cot):
    outs = [shape((TOKENS, HIDDEN), BF16)] + [shape(TOKEN, BF16)] * 8
    return pl.pallas_call(
        pair_kernel,
        out_shape=outs,
        in_specs=smem(1) + vmem(5),
        out_specs=vmem(len(outs)),
        compiler_params=params(NEAR_MB),
        cost_estimate=pl.CostEstimate(flops=20_000_000_000, bytes_accessed=2_000_000, transcendentals=0),
        name="pair",
    )(count, tok1, tok2, w_qkv, w_down, cot)


def run_front(core, counts, sectors, w_qkv, w_out, w_up, w_down, cot, near):
    outs = [
        shape(TOKEN, BF16),
        shape((16, 64, 640), BF16),
        shape((16, 64, 640), BF16),
        shape(TOKEN, F32),
        shape(TOKEN, BF16),
        shape(TOKEN, BF16),
        shape(TOKEN, BF16),
        shape(TOKEN, BF16),
        shape((6, GROUP, KEYS), BF16),
        shape(TOKEN, BF16),
    ]
    return pl.pallas_call(
        front_kernel,
        out_shape=outs,
        in_specs=smem(5) + vmem(7 + len(near)),
        out_specs=vmem(len(outs)),
        scratch_shapes=[
            pltpu.VMEM(TOKEN, BF16),
            pltpu.VMEM((4, TOKENS, 256), BF16),
            pltpu.VMEM((4, TOKENS, 128), BF16),
            pltpu.VMEM((2, TOKENS, 256), BF16),
        ],
        compiler_params=params(FRONT_MB),
        cost_estimate=pl.CostEstimate(flops=5_000_000_000, bytes_accessed=12_000_000, transcendentals=600_000),
        name="front",
    )(core, *counts, *sectors, w_qkv, w_out, w_up, w_down, cot, *near)


def run_back(core, saved):
    outs = [
        shape((16, 64, 384), BF16),
        shape((16, 64, 384), BF16),
        shape((4, TOKENS, 128), BF16),
        shape((4, 4 * TOKENS, 128), BF16),
        shape((4, 4 * TOKENS, 128), BF16),
    ]
    return pl.pallas_call(
        back_kernel,
        out_shape=outs,
        in_specs=smem(1) + vmem(len(saved)),
        out_specs=vmem(len(outs)),
        compiler_params=params(BACK_MB),
        cost_estimate=pl.CostEstimate(flops=6_000_000_000, bytes_accessed=12_000_000, transcendentals=0),
        name="back",
    )(core, *saved)


def run_push(w_qkv, grads):
    outs = [shape((2,) + TOKEN, BF16), shape(TOKEN, BF16), shape(TOKEN, F32)]
    return pl.pallas_call(
        push_kernel,
        out_shape=outs,
        in_specs=vmem(4),
        out_specs=vmem(3),
        compiler_params=params(NEAR_MB),
        cost_estimate=pl.CostEstimate(flops=2_000_000_000, bytes_accessed=4_000_000, transcendentals=0),
        name="push",
    )(w_qkv, *grads)


def small_call(kernel, outs, scalars, arrays, name):
    return pl.pallas_call(
        kernel,
        out_shape=outs,
        in_specs=smem(len(scalars)) + vmem(len(arrays)),
        out_specs=vmem(len(outs)),
        compiler_params=params(NEAR_MB),
        cost_estimate=pl.CostEstimate(flops=1_000_000, bytes_accessed=4_000_000, transcendentals=0),
        name=name,
    )(*scalars, *arrays)


def run_join(keep1, recv1, keep2, recv2, after):
    return pl.pallas_call(
        join_kernel,
        out_shape=shape((16, 64, 1024), BF16),
        in_specs=vmem(4) + [pl.BlockSpec(memory_space=pl.ANY)],
        out_specs=vmem(1)[0],
        compiler_params=params(NEAR_MB),
        cost_estimate=pl.CostEstimate(flops=1_000_000, bytes_accessed=4_000_000, transcendentals=0),
        name="join",
    )(keep1, recv1, keep2, recv2, after)


def run_add_x(*parts):
    return small_call(add_x_kernel, [shape(TOKEN, BF16)], [], parts, "add_x")[0]


def run_sum(parts):
    return small_call(sum_kernel, [shape((64, 1024), BF16)], [], [parts], "plane_sum")[0]


def run_finish(*parts):
    return small_call(finish_kernel, [shape(TOKEN, BF16), shape((8, 128), F32)], [], parts, "finish")


def run_final(lon, after, parts):
    outs = [shape((8, 1536), F32), shape((8, 512), F32), shape((8, 1024), F32), shape((16, 512), F32)]
    return pl.pallas_call(
        final_kernel,
        out_shape=outs,
        in_specs=smem(1) + vmem(5),
        out_specs=vmem(len(outs)),
        compiler_params=params(NEAR_MB),
        cost_estimate=pl.CostEstimate(flops=1_000_000, bytes_accessed=400_000, transcendentals=0),
        name="final",
    )(lon, after, *parts)


def sum_sources(values):
    return jnp.sum(values.astype(F32), axis=0).astype(BF16)


def swap(values):
    return lax.ppermute(values, "lon", CORE)


def local(tokens, ocean_count, w_qkv, w_out, w_up, w_down, cotangent):
    flat = tokens.reshape(TOKEN)
    cot = cotangent.reshape(TOKEN)
    tok2 = lax.ppermute(flat, "lon", X_LO)
    count = ocean_count.reshape(1, ROWS_DEV)
    count2 = lax.ppermute(count, "lon", X_LO)
    count1 = swap(count)
    lon = lax.axis_index("lon")
    core = (lon % 2).reshape(1)
    tok1 = swap(flat)
    query, inv_q, *own_kv = run_near(flat, w_qkv)
    tok3 = swap(tok2)
    grad_active, *pair = run_pair(count, tok1, tok2, w_qkv, w_down, cot)
    mate_kv, across_kv = pair[:4], pair[4:]
    count3 = swap(count2)
    front = run_front(
        core,
        (count, count1, count2, count3),
        (flat, tok3),
        w_qkv,
        w_out,
        w_up,
        w_down,
        cot,
        (query, *own_kv[1:3], *mate_kv[1:3], *across_kv[1:3], grad_active),
    )
    block_out, keep1, send1, grad_middle = front[:4]
    recv1 = swap(send1)
    saved = [query, inv_q] + [*own_kv, *mate_kv, *across_kv, *front[4:]]
    keep2, send2, *grads = run_back(core, saved)
    recv2 = swap(send2)
    for_core, for_x, grad_own = run_push(w_qkv, grads)
    joined = run_join(keep1, recv1, keep2, recv2, for_x)
    plane = lax.all_to_all(joined, ("lat", "lon"), 0, 0, axis_index_groups=PLANE_GROUPS, tiled=True)
    plane, for_x, for_core = lax.optimization_barrier((run_sum(plane), for_x, for_core))
    recv_core = swap(for_core)
    from_x = lax.ppermute(run_add_x(for_x, recv_core), "lon", X_LO)
    column = sum_sources(
        lax.all_to_all(plane.reshape(8, 8, 1024), "lat", 0, 0, axis_index_groups=Z_GROUPS, tiled=True)
    )
    gathered = [column] + [lax.ppermute(column, "lon", table) for table in (CORE, X_LO, DIAGONAL)]
    grad_tokens, done = run_finish(flat, grad_own, recv_core, from_x, grad_middle)
    weights = run_final(lon.reshape(1), done, gathered)
    return (block_out.reshape(tokens.shape), grad_tokens.reshape(tokens.shape), *weights)


def solution(mesh):
    in_specs = (P("lat", "lon", None), P("lat", "lon"), P(), P(), P(), P(), P("lat", "lon", None))
    out_specs = (
        P("lat", "lon", None),
        P("lat", "lon", None),
        P("lat", None),
        P("lat", None),
        P("lat", None),
        P("lat", None),
    )
    return jax.shard_map(local, mesh=mesh, in_specs=in_specs, out_specs=out_specs, check_vma=False)
```

```python
import math

import jax
import jax.numpy as jnp
from jax import lax
from jax.experimental import pallas as pl
from jax.experimental.pallas import tpu as pltpu
from jax.sharding import PartitionSpec as P

F32 = jnp.float32
BF16 = jnp.bfloat16
HEAD_DIM = 64
SOFTMAX_SCALE = 8.0
WIDTH = 512
HIDDEN = 1024
ROWS_DEV = 3
SECTOR = 64
TOKENS = ROWS_DEV * SECTOR
KEYS = 4 * SECTOR
GROUP = 256
GELU_A = math.sqrt(2.0 / math.pi)
GELU_B = 0.044715
NEAR_MB = 20
FRONT_MB = 28
BACK_MB = 28


def lat_index(z, y, x_hi):
    return (z * 4 + y) * 2 + x_hi


CORE = [(0, 1), (1, 0), (2, 3), (3, 2)]
X_LO = [(0, 2), (2, 0), (1, 3), (3, 1)]
DIAGONAL = [(0, 3), (3, 0), (1, 2), (2, 1)]
Z_ORDER = (0, 7, 1, 6, 2, 5, 3, 4)
Z_GROUPS = [[lat_index(z, y, x) for z in Z_ORDER] for y in range(4) for x in range(2)]
PLANE_GROUPS = [
    [
        lat_index(z, y, x_hi) * 4 + x_lo * 2 + core
        for y in reversed(range(4))
        for x_hi in reversed(range(2))
        for x_lo in reversed(range(2))
    ]
    for z in range(8)
    for core in range(2)
]


def mm(left, right):
    return lax.dot_general(left, right, (((1,), (0,)), ((), ())), preferred_element_type=F32)


def mm_nt(left, right):
    return lax.dot_general(left, right, (((1,), (1,)), ((), ())), preferred_element_type=F32)


def mm_tn(left, right):
    return lax.dot_general(left, right, (((0,), (0,)), ((), ())), preferred_element_type=F32)


def mean_last(values):
    return jnp.sum(values, axis=-1, keepdims=True) * (1.0 / values.shape[-1])


def layer_norm(values):
    centered = values - mean_last(values)
    inverse = lax.rsqrt(mean_last(centered * centered) + 1e-05)
    return centered * inverse, inverse


def layer_norm_back(normed, inverse, grad):
    return inverse * (grad - mean_last(grad) - normed * mean_last(grad * normed))


def head_blocks():
    same = lax.broadcasted_iota(jnp.int32, (GROUP, GROUP), 0) // HEAD_DIM == (
        lax.broadcasted_iota(jnp.int32, (GROUP, GROUP), 1) // HEAD_DIM
    )
    return jnp.where(same, 1.0, 0.0).astype(BF16)


def head_mean(values, blocks):
    parts = [
        mm(values[:, at : at + GROUP].astype(BF16), blocks) for at in range(0, values.shape[1], GROUP)
    ]
    return (parts[0] if len(parts) == 1 else jnp.concatenate(parts, axis=1)) * (1.0 / HEAD_DIM)


def head_masks(dtype):
    lane = lax.broadcasted_iota(jnp.int32, (1, GROUP), 1) // HEAD_DIM
    return [jnp.where(lane == head, 1.0, 0.0).astype(dtype) for head in range(4)]


def stack_heads(values, masks):
    return jnp.concatenate([values * mask for mask in masks], axis=0)


def unstack_heads(values, masks):
    return sum(values[head * SECTOR : (head + 1) * SECTOR] * masks[head] for head in range(4))


def store_pieces(out_ref, x_lo, column, product):
    width = product.shape[1]
    split = product.reshape(8, 8, 8, width)
    for place in range(8):
        piece = jnp.concatenate([split[z, place] for z in Z_ORDER], axis=0)
        out_ref[15 - place * 2 - x_lo, :, column : column + width] = piece.astype(BF16)


def rows_of(row, width=SECTOR):
    return slice(row * width, (row + 1) * width)


def key_value(tok_refs, w_qkv_ref, blocks, *out_refs):
    tokens = jnp.concatenate([ref[...] for ref in tok_refs], axis=0).astype(F32)
    normed = layer_norm(tokens)[0].astype(BF16)
    key_raw = mm(normed, w_qkv_ref[:, WIDTH : 2 * WIDTH])
    value = mm(normed, w_qkv_ref[:, 2 * WIDTH :]).astype(BF16)
    inv_k = lax.rsqrt(head_mean(key_raw * key_raw, blocks) + 1e-06)
    made = (normed, (key_raw * inv_k).astype(BF16), value, inv_k.astype(BF16))
    for at, ref in enumerate(out_refs):
        first = at // 4 * TOKENS
        ref[...] = made[at % 4][first : first + TOKENS]
    return normed


def own_mask(count_ref):
    place = lax.broadcasted_iota(jnp.int32, (SECTOR, 1), 0)
    return jnp.concatenate(
        [jnp.where(place < count_ref[0, row], 1.0, 0.0) for row in range(ROWS_DEV)], axis=0
    )


def near_kernel(tok0_ref, w_qkv_ref, query_ref, inv_q_ref, *own_refs):
    blocks = head_blocks()
    normed = key_value([tok0_ref], w_qkv_ref, blocks, *own_refs)
    query_raw = mm(normed, w_qkv_ref[:, :WIDTH])
    inv_q = lax.rsqrt(head_mean(query_raw * query_raw, blocks) + 1e-06)
    inv_q_ref[...] = inv_q.astype(BF16)
    query_ref[...] = (query_raw * inv_q).astype(BF16)


def active_kernel(count_ref, w_down_ref, cot_ref, grad_active_ref):
    branch = (own_mask(count_ref) * cot_ref[...].astype(F32)).astype(BF16)
    grad_active_ref[...] = mm_nt(branch, w_down_ref[...]).astype(BF16)


def pair_kernel(tok1_ref, tok2_ref, w_qkv_ref, *refs):
    key_value([tok1_ref, tok2_ref], w_qkv_ref, head_blocks(), *refs)


PLACES = [(row, slice(low, low + GROUP)) for row in range(ROWS_DEV) for low in (0, GROUP)]


def row_join(row, lanes, refs):
    return jnp.concatenate([ref[rows_of(row), lanes] for ref in refs], axis=0)


def front_kernel(
    core_ref,
    count_ref,
    count1_ref,
    count2_ref,
    count3_ref,
    tok0_ref,
    tok3_ref,
    w_qkv_ref,
    w_out_ref,
    w_up_ref,
    w_down_ref,
    cot_ref,
    query_ref,
    own_key_ref,
    own_value_ref,
    mate_key_ref,
    mate_value_ref,
    across_key_ref,
    across_value_ref,
    grad_active_ref,
    block_out_ref,
    keep_ref,
    send_ref,
    grad_middle_ref,
    normed_ref,
    key_ref,
    value_ref,
    inv_k_ref,
    probs_ref,
    grad_att_ref,
    att_ref,
    lift_ref,
    attn_ref,
    branch_ref,
    active_ref,
    glift_ref,
):
    blocks = head_blocks()
    masks_b = head_masks(BF16)
    masks_f = head_masks(F32)
    core = core_ref[0]
    key_value([tok3_ref], w_qkv_ref, blocks, normed_ref, key_ref, value_ref, inv_k_ref)
    key_refs = (own_key_ref, mate_key_ref, across_key_ref, key_ref)
    value_refs = (own_value_ref, mate_value_ref, across_value_ref, value_ref)

    key_place = lax.broadcasted_iota(jnp.int32, (1, KEYS), 1)
    key_masks = []
    for row in range(ROWS_DEV):
        limit = jnp.zeros((1, KEYS), jnp.int32)
        for sector, ref in enumerate((count_ref, count1_ref, count2_ref, count3_ref)):
            limit = jnp.where(key_place // SECTOR == sector, ref[0, row], limit)
        key_masks.append(jnp.where(key_place % SECTOR < limit, 1.0, 0.0))
    scores = [
        mm_nt(stack_heads(query_ref[rows_of(row), lanes], masks_b), row_join(row, lanes, key_refs))
        for row, lanes in PLACES
    ]
    for at, (row, lanes) in enumerate(PLACES):
        for head in range(4):
            some = rows_of(head)
            logits = scores[at][some] * (SOFTMAX_SCALE / HEAD_DIM) - SOFTMAX_SCALE
            expscore = jnp.exp(logits) * key_masks[row]
            total = jnp.sum(expscore, axis=1, keepdims=True)
            probs_ref[at, some, :] = (expscore * (1.0 / total)).astype(BF16)
    mixed = [mm(probs_ref[at], row_join(row, lanes, value_refs)) for at, (row, lanes) in enumerate(PLACES)]
    for at, (row, lanes) in enumerate(PLACES):
        att_ref[rows_of(row), lanes] = unstack_heads(mixed[at], masks_f).astype(BF16)

    mask = own_mask(count_ref)
    attended = att_ref[...]
    middle = tok0_ref[...].astype(F32) + mask * mm(attended, w_out_ref[...])
    normed_two, inverse = layer_norm(middle)
    normed_two_b = normed_two.astype(BF16)
    lifted = mm(normed_two_b, w_up_ref[...])
    for low in range(0, TOKENS, 48):
        rows = slice(low, low + 48)
        some = lifted[rows]
        square = some * some
        bent = jnp.tanh(GELU_A * some * (1.0 + GELU_B * square))
        half = 0.5 * (1.0 + bent)
        active_ref[rows, :] = (some * half).astype(BF16)
        slope = half + 0.5 * some * (1.0 - bent * bent) * (GELU_A * (1.0 + 3.0 * GELU_B * square))
        glift_ref[rows, :] = (slope * grad_active_ref[rows, :].astype(F32)).astype(BF16)
    active, grad_lifted = active_ref[...], glift_ref[...]
    branch = (mask * cot_ref[...].astype(F32)).astype(BF16)
    grad_normed = mm_nt(grad_lifted, w_up_ref[...])
    for part in range(2):
        branch_ref[part] = branch[:, part * 256 : (part + 1) * 256]
    for part in range(4):
        lift_ref[part] = grad_lifted[:, part * 256 : (part + 1) * 256]
    halves = ((keep_ref, core), (send_ref, 1 - core))
    active_t, normed_two_t = active.T, normed_two_b.T
    for out_ref, half_index in halves:
        term_down = mm(active_t, branch_ref[half_index]).reshape(64, 2, 8, 256)
        for x_lo in range(2):
            store_pieces(out_ref, x_lo, 384, term_down[:, x_lo].reshape(512, 256))
    grad_middle = cot_ref[...].astype(F32) + layer_norm_back(normed_two, inverse, grad_normed)
    grad_middle_ref[...] = grad_middle
    grad_attn = (mask * grad_middle).astype(BF16)
    grad_att_ref[...] = mm_nt(grad_attn, w_out_ref[...]).astype(BF16)
    block_out_ref[...] = (middle + mask * mm(active, w_down_ref[...])).astype(BF16)
    for out_ref, half_index in halves:
        for x_lo in range(2):
            store_pieces(out_ref, x_lo, 128, mm(normed_two_t, lift_ref[half_index + 2 * x_lo]))
    for part in range(4):
        attn_ref[part] = grad_attn[:, part * 128 : (part + 1) * 128]
    attended_t = attended.T
    for out_ref, half_index in halves:
        pair = jnp.concatenate([attn_ref[half_index], attn_ref[half_index + 2]], axis=1)
        term_out = mm(attended_t, pair)
        for x_lo in range(2):
            store_pieces(out_ref, x_lo, 0, term_out[:, x_lo * 128 : (x_lo + 1) * 128])


def norm_back(normed_b, inverse_b, grad, blocks):
    normed = normed_b.astype(F32)
    shift = head_mean(normed * grad, blocks)
    return (inverse_b.astype(F32) * (grad - normed * shift)).astype(BF16)


def qkv_half(out_ref, half_index, normed_refs, gq_ref, gk_ref, gv_ref):
    normed_all = jnp.concatenate([ref[...] for ref in normed_refs], axis=0)
    own_normed_t, normed_all_t = normed_refs[0][...].T, normed_all.T
    pair = jnp.concatenate([gq_ref[half_index], gq_ref[half_index + 2]], axis=1)
    term_q = mm(own_normed_t, pair)
    for x_lo in range(2):
        store_pieces(out_ref, x_lo, 0, term_q[:, x_lo * 128 : (x_lo + 1) * 128])
        pair = jnp.concatenate([gk_ref[half_index + 2 * x_lo], gv_ref[half_index + 2 * x_lo]], axis=1)
        store_pieces(out_ref, x_lo, 128, mm(normed_all_t, pair))


def back_kernel(core_ref, query_ref, inv_q_ref, *refs):
    sectors, (probs_ref, grad_att_ref, send_ref, gq_ref, gk_ref, gv_ref, scores_ref) = refs[:16], refs[16:]
    normed_refs, key_refs, value_refs, inv_k_refs = (sectors[at::4] for at in range(4))
    blocks = head_blocks()
    masks_b = head_masks(BF16)
    masks_f = head_masks(F32)
    stacked_q = [stack_heads(query_ref[rows_of(row), lanes], masks_b) for row, lanes in PLACES]
    stacked_g = [stack_heads(grad_att_ref[rows_of(row), lanes], masks_b) for row, lanes in PLACES]
    keys = [row_join(row, lanes, key_refs) for row, lanes in PLACES]
    grad_probs = [
        mm_nt(stacked_g[at], row_join(row, lanes, value_refs)) for at, (row, lanes) in enumerate(PLACES)
    ]
    for at in range(len(PLACES)):
        for head in range(4):
            some = rows_of(head)
            probs = probs_ref[at, some, :].astype(F32)
            grads = grad_probs[at][some]
            delta = jnp.sum(probs * grads, axis=1, keepdims=True)
            scores_ref[at, some, :] = (probs * (grads - delta) * (SOFTMAX_SCALE / HEAD_DIM)).astype(BF16)
    grad_scores = [scores_ref[at] for at in range(len(PLACES))]
    grad_v = [mm_tn(probs_ref[at], stacked_g[at]).astype(BF16) for at in range(len(PLACES))]
    grad_k = [mm_tn(grad_scores[at], stacked_q[at]) for at in range(len(PLACES))]
    grad_q = [unstack_heads(mm(grad_scores[at], keys[at]), masks_f) for at in range(len(PLACES))]
    for at, (row, lanes) in enumerate(PLACES):
        own = rows_of(row)
        back_q = norm_back(query_ref[own, lanes], inv_q_ref[own, lanes], grad_q[at], blocks)
        back_k = norm_back(keys[at], row_join(row, lanes, inv_k_refs), grad_k[at], blocks)
        for part in range(2):
            cut = slice(part * 128, (part + 1) * 128)
            quarter = lanes.start // 128 + part
            gq_ref[quarter, own, :] = back_q[:, cut]
            for ref, grad in ((gk_ref, back_k), (gv_ref, grad_v[at])):
                for sector in range(4):
                    rows = slice(sector * TOKENS + own.start, sector * TOKENS + own.stop)
                    ref[quarter, rows, :] = grad[sector * SECTOR : (sector + 1) * SECTOR, cut]

    qkv_half(send_ref, 1 - core_ref[0], normed_refs, gq_ref, gk_ref, gv_ref)


def push_kernel(core_ref, w_qkv_ref, gq_ref, gk_ref, gv_ref, *refs):
    normed_refs, (keep_ref, for_core_ref, for_x_ref, own_ref) = refs[:4], refs[4:]
    grad_q = jnp.concatenate([gq_ref[part] for part in range(4)], axis=1)
    grad_kv = jnp.concatenate([ref[part] for ref in (gk_ref, gv_ref) for part in range(4)], axis=1)
    grad_normed = mm_nt(grad_kv, w_qkv_ref[:, WIDTH:])
    for_core_ref[0] = grad_normed[TOKENS : 2 * TOKENS].astype(BF16)
    for_x_ref[...] = grad_normed[2 * TOKENS : 3 * TOKENS].astype(BF16)
    for_core_ref[1] = grad_normed[3 * TOKENS :].astype(BF16)
    own_ref[...] = grad_normed[:TOKENS] + mm_nt(grad_q, w_qkv_ref[:, :WIDTH])
    qkv_half(keep_ref, core_ref[0], normed_refs, gq_ref, gk_ref, gv_ref)


def join_kernel(keep1_ref, recv1_ref, keep2_ref, recv2_ref, after_ref, out_ref):
    del after_ref
    for piece in range(16):
        out_ref[piece, :, :384] = (keep2_ref[piece].astype(F32) + recv2_ref[piece].astype(F32)).astype(BF16)
        out_ref[piece, :, 384:] = (keep1_ref[piece].astype(F32) + recv1_ref[piece].astype(F32)).astype(BF16)


def add_x_kernel(for_x_ref, recv_core_ref, out_ref):
    out_ref[...] = (for_x_ref[...].astype(F32) + recv_core_ref[1].astype(F32)).astype(BF16)


def sum_kernel(parts_ref, out_ref):
    for low in range(0, out_ref.shape[0], 16):
        rows = slice(low, low + 16)
        total = parts_ref[0, rows, :].astype(F32)
        for part in range(1, parts_ref.shape[0]):
            total = total + parts_ref[part, rows, :].astype(F32)
        out_ref[rows, :] = total.astype(BF16)


def finish_kernel(tok_ref, own_ref, recv_core_ref, from_x_ref, middle_ref, out_ref, done_ref):
    done_ref[...] = jnp.zeros((8, 128), F32)
    grad = own_ref[...] + recv_core_ref[0].astype(F32) + from_x_ref[...].astype(F32)
    normed, inverse = layer_norm(tok_ref[...].astype(F32))
    out_ref[...] = (middle_ref[...] + layer_norm_back(normed, inverse, grad)).astype(BF16)


def final_kernel(lon_ref, after_ref, own_ref, core_ref, x_ref, diagonal_ref, qkv_ref, out_ref, up_ref, down_ref):
    del after_ref
    lon = lon_ref[0]
    scale = 1.0 / math.sqrt(64 * 4 * TOKENS)
    held = [ref[...].astype(F32) * scale for ref in (own_ref, core_ref, x_ref, diagonal_ref)]
    for quarter in range(4):
        part = held[3]
        for distance in range(3):
            part = jnp.where(lon == (quarter ^ distance), held[distance], part)
        at = slice(quarter * 128, (quarter + 1) * 128)
        for matrix in range(3):
            low = matrix * WIDTH + quarter * 128
            qkv_ref[:, low : low + 128] = part[:, matrix * 128 : (matrix + 1) * 128]
        out_ref[:, at] = part[:, 384:512]
        up_ref[:, quarter * 256 : (quarter + 1) * 256] = part[:, 512:768]
        side = (quarter % 2) * 256
        down_ref[(quarter // 2) * 8 : (quarter // 2) * 8 + 8, side : side + 256] = part[:, 768:]


def vmem(count):
    return [pl.BlockSpec(memory_space=pltpu.VMEM)] * count


def smem(count):
    return [pl.BlockSpec(memory_space=pltpu.SMEM)] * count


def shape(dims, dtype):
    return jax.ShapeDtypeStruct(dims, dtype)


TOKEN = (TOKENS, WIDTH)


def params(megabytes):
    return pltpu.CompilerParams(vmem_limit_bytes=megabytes * 1024 * 1024)


def run_near(tok0, w_qkv):
    outs = [shape(TOKEN, BF16)] * 6
    return pl.pallas_call(
        near_kernel,
        out_shape=outs,
        in_specs=vmem(2),
        out_specs=vmem(len(outs)),
        compiler_params=params(NEAR_MB),
        cost_estimate=pl.CostEstimate(flops=2_500_000_000, bytes_accessed=4_000_000, transcendentals=0),
        name="near",
    )(tok0, w_qkv)


def run_active(count, w_down, cot):
    return pl.pallas_call(
        active_kernel,
        out_shape=shape((TOKENS, HIDDEN), BF16),
        in_specs=smem(1) + vmem(2),
        out_specs=vmem(1)[0],
        compiler_params=params(NEAR_MB),
        cost_estimate=pl.CostEstimate(flops=2_500_000_000, bytes_accessed=2_000_000, transcendentals=0),
        name="active",
    )(count, w_down, cot)


def run_pair(tok1, tok2, w_qkv):
    outs = [shape(TOKEN, BF16)] * 8
    return pl.pallas_call(
        pair_kernel,
        out_shape=outs,
        in_specs=vmem(3),
        out_specs=vmem(len(outs)),
        compiler_params=params(NEAR_MB),
        cost_estimate=pl.CostEstimate(flops=20_000_000_000, bytes_accessed=2_000_000, transcendentals=0),
        name="pair",
    )(tok1, tok2, w_qkv)


def run_front(core, counts, sectors, w_qkv, w_out, w_up, w_down, cot, near):
    outs = [
        shape(TOKEN, BF16),
        shape((16, 64, 640), BF16),
        shape((16, 64, 640), BF16),
        shape(TOKEN, F32),
        shape(TOKEN, BF16),
        shape(TOKEN, BF16),
        shape(TOKEN, BF16),
        shape(TOKEN, BF16),
        shape((6, GROUP, KEYS), BF16),
        shape(TOKEN, BF16),
    ]
    return pl.pallas_call(
        front_kernel,
        out_shape=outs,
        in_specs=smem(5) + vmem(7 + len(near)),
        out_specs=vmem(len(outs)),
        scratch_shapes=[
            pltpu.VMEM(TOKEN, BF16),
            pltpu.VMEM((4, TOKENS, 256), BF16),
            pltpu.VMEM((4, TOKENS, 128), BF16),
            pltpu.VMEM((2, TOKENS, 256), BF16),
            pltpu.VMEM((TOKENS, HIDDEN), BF16),
            pltpu.VMEM((TOKENS, HIDDEN), BF16),
        ],
        compiler_params=params(FRONT_MB),
        cost_estimate=pl.CostEstimate(flops=5_000_000_000, bytes_accessed=12_000_000, transcendentals=600_000),
        name="front",
    )(core, *counts, *sectors, w_qkv, w_out, w_up, w_down, cot, *near)


def run_back(core, saved):
    outs = [
        shape((16, 64, 384), BF16),
        shape((4, TOKENS, 128), BF16),
        shape((4, 4 * TOKENS, 128), BF16),
        shape((4, 4 * TOKENS, 128), BF16),
    ]
    return pl.pallas_call(
        back_kernel,
        out_shape=outs,
        in_specs=smem(1) + vmem(len(saved)),
        out_specs=vmem(len(outs)),
        scratch_shapes=[pltpu.VMEM((6, GROUP, KEYS), BF16)],
        compiler_params=params(BACK_MB),
        cost_estimate=pl.CostEstimate(flops=6_000_000_000, bytes_accessed=12_000_000, transcendentals=0),
        name="back",
    )(core, *saved)


def run_push(core, w_qkv, grads, normed):
    outs = [shape((16, 64, 384), BF16), shape((2,) + TOKEN, BF16), shape(TOKEN, BF16), shape(TOKEN, F32)]
    return pl.pallas_call(
        push_kernel,
        out_shape=outs,
        in_specs=smem(1) + vmem(8),
        out_specs=vmem(4),
        compiler_params=params(BACK_MB),
        cost_estimate=pl.CostEstimate(flops=2_000_000_000, bytes_accessed=4_000_000, transcendentals=0),
        name="push",
    )(core, w_qkv, *grads, *normed)


def small_call(kernel, outs, scalars, arrays, name):
    return pl.pallas_call(
        kernel,
        out_shape=outs,
        in_specs=smem(len(scalars)) + vmem(len(arrays)),
        out_specs=vmem(len(outs)),
        compiler_params=params(NEAR_MB),
        cost_estimate=pl.CostEstimate(flops=1_000_000, bytes_accessed=4_000_000, transcendentals=0),
        name=name,
    )(*scalars, *arrays)


def run_join(keep1, recv1, keep2, recv2, after):
    return pl.pallas_call(
        join_kernel,
        out_shape=shape((16, 64, 1024), BF16),
        in_specs=vmem(4) + [pl.BlockSpec(memory_space=pl.ANY)],
        out_specs=vmem(1)[0],
        compiler_params=params(NEAR_MB),
        cost_estimate=pl.CostEstimate(flops=1_000_000, bytes_accessed=4_000_000, transcendentals=0),
        name="join",
    )(keep1, recv1, keep2, recv2, after)


def run_add_x(*parts):
    return small_call(add_x_kernel, [shape(TOKEN, BF16)], [], parts, "add_x")[0]


def run_sum(parts):
    return small_call(sum_kernel, [shape((64, 1024), BF16)], [], [parts], "plane_sum")[0]


def run_finish(*parts):
    return small_call(finish_kernel, [shape(TOKEN, BF16), shape((8, 128), F32)], [], parts, "finish")


def run_final(lon, after, parts):
    outs = [shape((8, 1536), F32), shape((8, 512), F32), shape((8, 1024), F32), shape((16, 512), F32)]
    return pl.pallas_call(
        final_kernel,
        out_shape=outs,
        in_specs=smem(1) + vmem(5),
        out_specs=vmem(len(outs)),
        compiler_params=params(NEAR_MB),
        cost_estimate=pl.CostEstimate(flops=1_000_000, bytes_accessed=400_000, transcendentals=0),
        name="final",
    )(lon, after, *parts)


def sum_sources(values):
    return jnp.sum(values.astype(F32), axis=0).astype(BF16)


def swap(values):
    return lax.ppermute(values, "lon", CORE)


def local(tokens, ocean_count, w_qkv, w_out, w_up, w_down, cotangent):
    flat = tokens.reshape(TOKEN)
    cot = cotangent.reshape(TOKEN)
    tok2 = lax.ppermute(flat, "lon", X_LO)
    count = ocean_count.reshape(1, ROWS_DEV)
    count2 = lax.ppermute(count, "lon", X_LO)
    count1 = swap(count)
    lon = lax.axis_index("lon")
    core = (lon % 2).reshape(1)
    tok1 = swap(flat)
    query, inv_q, *own_kv = run_near(flat, w_qkv)
    tok3 = swap(tok2)
    grad_active = run_active(count, w_down, cot)
    pair = run_pair(tok1, tok2, w_qkv)
    mate_kv, across_kv = pair[:4], pair[4:]
    count3 = swap(count2)
    front = run_front(
        core,
        (count, count1, count2, count3),
        (flat, tok3),
        w_qkv,
        w_out,
        w_up,
        w_down,
        cot,
        (query, *own_kv[1:3], *mate_kv[1:3], *across_kv[1:3], grad_active),
    )
    block_out, keep1, send1, grad_middle = front[:4]
    recv1 = swap(send1)
    saved = [query, inv_q] + [*own_kv, *mate_kv, *across_kv, *front[4:]]
    send2, *grads = run_back(core, saved)
    recv2 = swap(send2)
    normed = [own_kv[0], mate_kv[0], across_kv[0], front[4]]
    keep2, for_core, for_x, grad_own = run_push(core, w_qkv, grads, normed)
    joined = run_join(keep1, recv1, keep2, recv2, for_x)
    plane = lax.all_to_all(joined, ("lat", "lon"), 0, 0, axis_index_groups=PLANE_GROUPS, tiled=True)
    plane, for_x, for_core = lax.optimization_barrier((run_sum(plane), for_x, for_core))
    recv_core = swap(for_core)
    from_x = lax.ppermute(run_add_x(for_x, recv_core), "lon", X_LO)
    column = sum_sources(
        lax.all_to_all(plane.reshape(8, 8, 1024), "lat", 0, 0, axis_index_groups=Z_GROUPS, tiled=True)
    )
    gathered = [column] + [lax.ppermute(column, "lon", table) for table in (CORE, X_LO, DIAGONAL)]
    grad_tokens, done = run_finish(flat, grad_own, recv_core, from_x, grad_middle)
    weights = run_final(lon.reshape(1), done, gathered)
    return (block_out.reshape(tokens.shape), grad_tokens.reshape(tokens.shape), *weights)


def solution(mesh):
    in_specs = (P("lat", "lon", None), P("lat", "lon"), P(), P(), P(), P(), P("lat", "lon", None))
    out_specs = (
        P("lat", "lon", None),
        P("lat", "lon", None),
        P("lat", None),
        P("lat", None),
        P("lat", None),
        P("lat", None),
    )
    return jax.shard_map(local, mesh=mesh, in_specs=in_specs, out_specs=out_specs, check_vma=False)
```

```python
import math

import jax
import jax.numpy as jnp
from jax import lax
from jax.experimental import pallas as pl
from jax.experimental.pallas import tpu as pltpu
from jax.sharding import PartitionSpec as P

F32 = jnp.float32
BF16 = jnp.bfloat16
HEAD_DIM = 64
SOFTMAX_SCALE = 8.0
WIDTH = 512
HIDDEN = 1024
ROWS_DEV = 3
SECTOR = 64
TOKENS = ROWS_DEV * SECTOR
KEYS = 4 * SECTOR
GROUP = 256
GELU_A = math.sqrt(2.0 / math.pi)
GELU_B = 0.044715
NEAR_MB = 20
FRONT_MB = 28
BACK_MB = 28


def lat_index(z, y, x_hi):
    return (z * 4 + y) * 2 + x_hi


CORE = [(0, 1), (1, 0), (2, 3), (3, 2)]
X_LO = [(0, 2), (2, 0), (1, 3), (3, 1)]
DIAGONAL = [(0, 3), (3, 0), (1, 2), (2, 1)]
Z_ORDER = (4, 3, 5, 2, 6, 1, 7, 0)
Z_GROUPS = [[lat_index(z, y, x) for z in Z_ORDER] for y in range(4) for x in range(2)]
PLANE_GROUPS = [
    [
        lat_index(z, y, x_hi) * 4 + x_lo * 2 + core
        for y in reversed(range(4))
        for x_hi in reversed(range(2))
        for x_lo in reversed(range(2))
    ]
    for z in range(8)
    for core in range(2)
]


def mm(left, right):
    return lax.dot_general(left, right, (((1,), (0,)), ((), ())), preferred_element_type=F32)


def mm_nt(left, right):
    return lax.dot_general(left, right, (((1,), (1,)), ((), ())), preferred_element_type=F32)


def mm_tn(left, right):
    return lax.dot_general(left, right, (((0,), (0,)), ((), ())), preferred_element_type=F32)


def mean_last(values):
    return jnp.sum(values, axis=-1, keepdims=True) * (1.0 / values.shape[-1])


def layer_norm(values):
    centered = values - mean_last(values)
    inverse = lax.rsqrt(mean_last(centered * centered) + 1e-05)
    return centered * inverse, inverse


def layer_norm_back(normed, inverse, grad):
    return inverse * (grad - mean_last(grad) - normed * mean_last(grad * normed))


def head_blocks():
    same = lax.broadcasted_iota(jnp.int32, (GROUP, GROUP), 0) // HEAD_DIM == (
        lax.broadcasted_iota(jnp.int32, (GROUP, GROUP), 1) // HEAD_DIM
    )
    return jnp.where(same, 1.0, 0.0).astype(BF16)


def head_mean(values, blocks):
    parts = [
        mm(values[:, at : at + GROUP].astype(BF16), blocks) for at in range(0, values.shape[1], GROUP)
    ]
    return (parts[0] if len(parts) == 1 else jnp.concatenate(parts, axis=1)) * (1.0 / HEAD_DIM)


def head_masks(dtype):
    lane = lax.broadcasted_iota(jnp.int32, (1, GROUP), 1) // HEAD_DIM
    return [jnp.where(lane == head, 1.0, 0.0).astype(dtype) for head in range(4)]


def stack_heads(values, masks):
    return jnp.concatenate([values * mask for mask in masks], axis=0)


def unstack_heads(values, masks):
    return sum(values[head * SECTOR : (head + 1) * SECTOR] * masks[head] for head in range(4))


def store_pieces(out_ref, x_lo, column, product):
    width = product.shape[1]
    split = product.reshape(8, 8, 8, width)
    for place in range(8):
        piece = jnp.concatenate([split[z, place] for z in Z_ORDER], axis=0)
        out_ref[15 - place * 2 - x_lo, :, column : column + width] = piece.astype(BF16)


def rows_of(row, width=SECTOR):
    return slice(row * width, (row + 1) * width)


def key_value(tok_refs, w_qkv_ref, blocks, *out_refs):
    tokens = jnp.concatenate([ref[...] for ref in tok_refs], axis=0).astype(F32)
    normed = layer_norm(tokens)[0].astype(BF16)
    key_raw = mm(normed, w_qkv_ref[:, WIDTH : 2 * WIDTH])
    value = mm(normed, w_qkv_ref[:, 2 * WIDTH :]).astype(BF16)
    inv_k = lax.rsqrt(head_mean(key_raw * key_raw, blocks) + 1e-06)
    made = (normed, (key_raw * inv_k).astype(BF16), value, inv_k.astype(BF16))
    for at, ref in enumerate(out_refs):
        first = at // 4 * TOKENS
        ref[...] = made[at % 4][first : first + TOKENS]
    return normed


def own_mask(count_ref):
    place = lax.broadcasted_iota(jnp.int32, (SECTOR, 1), 0)
    return jnp.concatenate(
        [jnp.where(place < count_ref[0, row], 1.0, 0.0) for row in range(ROWS_DEV)], axis=0
    )


def near_kernel(tok0_ref, w_qkv_ref, query_ref, inv_q_ref, *own_refs):
    blocks = head_blocks()
    normed = key_value([tok0_ref], w_qkv_ref, blocks, *own_refs)
    query_raw = mm(normed, w_qkv_ref[:, :WIDTH])
    inv_q = lax.rsqrt(head_mean(query_raw * query_raw, blocks) + 1e-06)
    inv_q_ref[...] = inv_q.astype(BF16)
    query_ref[...] = (query_raw * inv_q).astype(BF16)


def active_kernel(count_ref, w_down_ref, cot_ref, grad_active_ref):
    branch = (own_mask(count_ref) * cot_ref[...].astype(F32)).astype(BF16)
    grad_active_ref[...] = mm_nt(branch, w_down_ref[...]).astype(BF16)


def pair_kernel(tok1_ref, tok2_ref, w_qkv_ref, *refs):
    key_value([tok1_ref, tok2_ref], w_qkv_ref, head_blocks(), *refs)


PLACES = [(row, slice(low, low + GROUP)) for row in range(ROWS_DEV) for low in (0, GROUP)]


def row_join(row, lanes, refs):
    return jnp.concatenate([ref[rows_of(row), lanes] for ref in refs], axis=0)


def front_kernel(
    core_ref,
    count_ref,
    count1_ref,
    count2_ref,
    count3_ref,
    tok0_ref,
    tok3_ref,
    w_qkv_ref,
    w_out_ref,
    w_up_ref,
    w_down_ref,
    cot_ref,
    query_ref,
    own_key_ref,
    own_value_ref,
    mate_key_ref,
    mate_value_ref,
    across_key_ref,
    across_value_ref,
    grad_active_ref,
    block_out_ref,
    keep_ref,
    send_ref,
    grad_middle_ref,
    normed_ref,
    key_ref,
    value_ref,
    inv_k_ref,
    probs_ref,
    grad_att_ref,
    att_ref,
    lift_ref,
    attn_ref,
    branch_ref,
    active_ref,
    glift_ref,
):
    blocks = head_blocks()
    masks_b = head_masks(BF16)
    masks_f = head_masks(F32)
    core = core_ref[0]
    key_value([tok3_ref], w_qkv_ref, blocks, normed_ref, key_ref, value_ref, inv_k_ref)
    key_refs = (own_key_ref, mate_key_ref, across_key_ref, key_ref)
    value_refs = (own_value_ref, mate_value_ref, across_value_ref, value_ref)

    key_place = lax.broadcasted_iota(jnp.int32, (1, KEYS), 1)
    key_masks = []
    for row in range(ROWS_DEV):
        limit = jnp.zeros((1, KEYS), jnp.int32)
        for sector, ref in enumerate((count_ref, count1_ref, count2_ref, count3_ref)):
            limit = jnp.where(key_place // SECTOR == sector, ref[0, row], limit)
        key_masks.append(jnp.where(key_place % SECTOR < limit, 1.0, 0.0))
    scores = [
        mm_nt(stack_heads(query_ref[rows_of(row), lanes], masks_b), row_join(row, lanes, key_refs))
        for row, lanes in PLACES
    ]
    for at, (row, lanes) in enumerate(PLACES):
        for head in range(4):
            some = rows_of(head)
            logits = scores[at][some] * (SOFTMAX_SCALE / HEAD_DIM) - SOFTMAX_SCALE
            expscore = jnp.exp(logits) * key_masks[row]
            total = jnp.sum(expscore, axis=1, keepdims=True)
            probs_ref[at, some, :] = (expscore * (1.0 / total)).astype(BF16)
    mixed = [mm(probs_ref[at], row_join(row, lanes, value_refs)) for at, (row, lanes) in enumerate(PLACES)]
    for at, (row, lanes) in enumerate(PLACES):
        att_ref[rows_of(row), lanes] = unstack_heads(mixed[at], masks_f).astype(BF16)

    mask = own_mask(count_ref)
    attended = att_ref[...]
    middle = tok0_ref[...].astype(F32) + mask * mm(attended, w_out_ref[...])
    normed_two, inverse = layer_norm(middle)
    normed_two_b = normed_two.astype(BF16)
    lifted = mm(normed_two_b, w_up_ref[...])
    for low in range(0, TOKENS, 48):
        rows = slice(low, low + 48)
        some = lifted[rows]
        square = some * some
        bent = jnp.tanh(GELU_A * some * (1.0 + GELU_B * square))
        half = 0.5 * (1.0 + bent)
        active_ref[rows, :] = (some * half).astype(BF16)
        slope = half + 0.5 * some * (1.0 - bent * bent) * (GELU_A * (1.0 + 3.0 * GELU_B * square))
        glift_ref[rows, :] = (slope * grad_active_ref[rows, :].astype(F32)).astype(BF16)
    active, grad_lifted = active_ref[...], glift_ref[...]
    branch = (mask * cot_ref[...].astype(F32)).astype(BF16)
    grad_normed = mm_nt(grad_lifted, w_up_ref[...])
    for part in range(2):
        branch_ref[part] = branch[:, part * 256 : (part + 1) * 256]
    for part in range(4):
        lift_ref[part] = grad_lifted[:, part * 256 : (part + 1) * 256]
    halves = ((keep_ref, core), (send_ref, 1 - core))
    active_t, normed_two_t = active.T, normed_two_b.T
    for out_ref, half_index in halves:
        term_down = mm(active_t, branch_ref[half_index]).reshape(64, 2, 8, 256)
        for x_lo in range(2):
            store_pieces(out_ref, x_lo, 384, term_down[:, x_lo].reshape(512, 256))
    grad_middle = cot_ref[...].astype(F32) + layer_norm_back(normed_two, inverse, grad_normed)
    grad_middle_ref[...] = grad_middle
    grad_attn = (mask * grad_middle).astype(BF16)
    grad_att_ref[...] = mm_nt(grad_attn, w_out_ref[...]).astype(BF16)
    block_out_ref[...] = (middle + mask * mm(active, w_down_ref[...])).astype(BF16)
    for out_ref, half_index in halves:
        for x_lo in range(2):
            store_pieces(out_ref, x_lo, 128, mm(normed_two_t, lift_ref[half_index + 2 * x_lo]))
    for part in range(4):
        attn_ref[part] = grad_attn[:, part * 128 : (part + 1) * 128]
    attended_t = attended.T
    for out_ref, half_index in halves:
        pair = jnp.concatenate([attn_ref[half_index], attn_ref[half_index + 2]], axis=1)
        term_out = mm(attended_t, pair)
        for x_lo in range(2):
            store_pieces(out_ref, x_lo, 0, term_out[:, x_lo * 128 : (x_lo + 1) * 128])


def norm_back(normed_b, inverse_b, grad, blocks):
    normed = normed_b.astype(F32)
    shift = head_mean(normed * grad, blocks)
    return (inverse_b.astype(F32) * (grad - normed * shift)).astype(BF16)


def qkv_half(out_ref, half_index, normed_refs, gq_ref, gk_ref, gv_ref):
    normed_all = jnp.concatenate([ref[...] for ref in normed_refs], axis=0)
    own_normed_t, normed_all_t = normed_refs[0][...].T, normed_all.T
    pair = jnp.concatenate([gq_ref[half_index], gq_ref[half_index + 2]], axis=1)
    term_q = mm(own_normed_t, pair)
    for x_lo in range(2):
        store_pieces(out_ref, x_lo, 0, term_q[:, x_lo * 128 : (x_lo + 1) * 128])
        pair = jnp.concatenate([gk_ref[half_index + 2 * x_lo], gv_ref[half_index + 2 * x_lo]], axis=1)
        store_pieces(out_ref, x_lo, 128, mm(normed_all_t, pair))


def back_kernel(core_ref, query_ref, inv_q_ref, *refs):
    sectors, (probs_ref, grad_att_ref, send_ref, gq_ref, gk_ref, gv_ref, scores_ref) = refs[:16], refs[16:]
    normed_refs, key_refs, value_refs, inv_k_refs = (sectors[at::4] for at in range(4))
    blocks = head_blocks()
    masks_b = head_masks(BF16)
    masks_f = head_masks(F32)
    stacked_q = [stack_heads(query_ref[rows_of(row), lanes], masks_b) for row, lanes in PLACES]
    stacked_g = [stack_heads(grad_att_ref[rows_of(row), lanes], masks_b) for row, lanes in PLACES]
    keys = [row_join(row, lanes, key_refs) for row, lanes in PLACES]
    grad_probs = [
        mm_nt(stacked_g[at], row_join(row, lanes, value_refs)) for at, (row, lanes) in enumerate(PLACES)
    ]
    for at in range(len(PLACES)):
        for head in range(4):
            some = rows_of(head)
            probs = probs_ref[at, some, :].astype(F32)
            grads = grad_probs[at][some]
            delta = jnp.sum(probs * grads, axis=1, keepdims=True)
            scores_ref[at, some, :] = (probs * (grads - delta) * (SOFTMAX_SCALE / HEAD_DIM)).astype(BF16)
    grad_scores = [scores_ref[at] for at in range(len(PLACES))]
    grad_v = [mm_tn(probs_ref[at], stacked_g[at]).astype(BF16) for at in range(len(PLACES))]
    grad_k = [mm_tn(grad_scores[at], stacked_q[at]) for at in range(len(PLACES))]
    grad_q = [unstack_heads(mm(grad_scores[at], keys[at]), masks_f) for at in range(len(PLACES))]
    for at, (row, lanes) in enumerate(PLACES):
        own = rows_of(row)
        back_q = norm_back(query_ref[own, lanes], inv_q_ref[own, lanes], grad_q[at], blocks)
        back_k = norm_back(keys[at], row_join(row, lanes, inv_k_refs), grad_k[at], blocks)
        for part in range(2):
            cut = slice(part * 128, (part + 1) * 128)
            quarter = lanes.start // 128 + part
            gq_ref[quarter, own, :] = back_q[:, cut]
            for ref, grad in ((gk_ref, back_k), (gv_ref, grad_v[at])):
                for sector in range(4):
                    rows = slice(sector * TOKENS + own.start, sector * TOKENS + own.stop)
                    ref[quarter, rows, :] = grad[sector * SECTOR : (sector + 1) * SECTOR, cut]

    qkv_half(send_ref, 1 - core_ref[0], normed_refs, gq_ref, gk_ref, gv_ref)


def push_kernel(core_ref, w_qkv_ref, gq_ref, gk_ref, gv_ref, *refs):
    normed_refs, (keep_ref, for_core_ref, for_x_ref, own_ref) = refs[:4], refs[4:]
    grad_q = jnp.concatenate([gq_ref[part] for part in range(4)], axis=1)
    grad_kv = jnp.concatenate([ref[part] for ref in (gk_ref, gv_ref) for part in range(4)], axis=1)
    grad_normed = mm_nt(grad_kv, w_qkv_ref[:, WIDTH:])
    for_core_ref[0] = grad_normed[TOKENS : 2 * TOKENS].astype(BF16)
    for_x_ref[...] = grad_normed[2 * TOKENS : 3 * TOKENS].astype(BF16)
    for_core_ref[1] = grad_normed[3 * TOKENS :].astype(BF16)
    own_ref[...] = grad_normed[:TOKENS] + mm_nt(grad_q, w_qkv_ref[:, :WIDTH])
    qkv_half(keep_ref, core_ref[0], normed_refs, gq_ref, gk_ref, gv_ref)


def join_kernel(keep1_ref, recv1_ref, keep2_ref, recv2_ref, after_ref, out_ref):
    del after_ref
    for piece in range(16):
        out_ref[piece, :, :384] = (keep2_ref[piece].astype(F32) + recv2_ref[piece].astype(F32)).astype(BF16)
        out_ref[piece, :, 384:] = (keep1_ref[piece].astype(F32) + recv1_ref[piece].astype(F32)).astype(BF16)


def add_x_kernel(for_x_ref, recv_core_ref, out_ref):
    out_ref[...] = (for_x_ref[...].astype(F32) + recv_core_ref[1].astype(F32)).astype(BF16)


def sum_kernel(parts_ref, out_ref):
    for low in range(0, out_ref.shape[0], 16):
        rows = slice(low, low + 16)
        total = parts_ref[0, rows, :].astype(F32)
        for part in range(1, parts_ref.shape[0]):
            total = total + parts_ref[part, rows, :].astype(F32)
        out_ref[rows, :] = total.astype(BF16)


def finish_kernel(tok_ref, own_ref, recv_core_ref, from_x_ref, middle_ref, out_ref, done_ref):
    done_ref[...] = jnp.zeros((8, 128), F32)
    grad = own_ref[...] + recv_core_ref[0].astype(F32) + from_x_ref[...].astype(F32)
    normed, inverse = layer_norm(tok_ref[...].astype(F32))
    out_ref[...] = (middle_ref[...] + layer_norm_back(normed, inverse, grad)).astype(BF16)


def final_kernel(lon_ref, after_ref, own_ref, core_ref, x_ref, diagonal_ref, qkv_ref, out_ref, up_ref, down_ref):
    del after_ref
    lon = lon_ref[0]
    scale = 1.0 / math.sqrt(64 * 4 * TOKENS)
    held = [ref[...].astype(F32) * scale for ref in (own_ref, core_ref, x_ref, diagonal_ref)]
    for quarter in range(4):
        part = held[3]
        for distance in range(3):
            part = jnp.where(lon == (quarter ^ distance), held[distance], part)
        at = slice(quarter * 128, (quarter + 1) * 128)
        for matrix in range(3):
            low = matrix * WIDTH + quarter * 128
            qkv_ref[:, low : low + 128] = part[:, matrix * 128 : (matrix + 1) * 128]
        out_ref[:, at] = part[:, 384:512]
        up_ref[:, quarter * 256 : (quarter + 1) * 256] = part[:, 512:768]
        side = (quarter % 2) * 256
        down_ref[(quarter // 2) * 8 : (quarter // 2) * 8 + 8, side : side + 256] = part[:, 768:]


def vmem(count):
    return [pl.BlockSpec(memory_space=pltpu.VMEM)] * count


def smem(count):
    return [pl.BlockSpec(memory_space=pltpu.SMEM)] * count


def shape(dims, dtype):
    return jax.ShapeDtypeStruct(dims, dtype)


TOKEN = (TOKENS, WIDTH)


def params(megabytes):
    return pltpu.CompilerParams(vmem_limit_bytes=megabytes * 1024 * 1024)


def run_near(tok0, w_qkv):
    outs = [shape(TOKEN, BF16)] * 6
    return pl.pallas_call(
        near_kernel,
        out_shape=outs,
        in_specs=vmem(2),
        out_specs=vmem(len(outs)),
        compiler_params=params(NEAR_MB),
        cost_estimate=pl.CostEstimate(flops=2_500_000_000, bytes_accessed=4_000_000, transcendentals=0),
        name="near",
    )(tok0, w_qkv)


def run_active(count, w_down, cot):
    return pl.pallas_call(
        active_kernel,
        out_shape=shape((TOKENS, HIDDEN), BF16),
        in_specs=smem(1) + vmem(2),
        out_specs=vmem(1)[0],
        compiler_params=params(NEAR_MB),
        cost_estimate=pl.CostEstimate(flops=2_500_000_000, bytes_accessed=2_000_000, transcendentals=0),
        name="active",
    )(count, w_down, cot)


def run_pair(tok1, tok2, w_qkv):
    outs = [shape(TOKEN, BF16)] * 8
    return pl.pallas_call(
        pair_kernel,
        out_shape=outs,
        in_specs=vmem(3),
        out_specs=vmem(len(outs)),
        compiler_params=params(NEAR_MB),
        cost_estimate=pl.CostEstimate(flops=20_000_000_000, bytes_accessed=2_000_000, transcendentals=0),
        name="pair",
    )(tok1, tok2, w_qkv)


def run_front(core, counts, sectors, w_qkv, w_out, w_up, w_down, cot, near):
    outs = [
        shape(TOKEN, BF16),
        shape((16, 64, 640), BF16),
        shape((16, 64, 640), BF16),
        shape(TOKEN, F32),
        shape(TOKEN, BF16),
        shape(TOKEN, BF16),
        shape(TOKEN, BF16),
        shape(TOKEN, BF16),
        shape((6, GROUP, KEYS), BF16),
        shape(TOKEN, BF16),
    ]
    return pl.pallas_call(
        front_kernel,
        out_shape=outs,
        in_specs=smem(5) + vmem(7 + len(near)),
        out_specs=vmem(len(outs)),
        scratch_shapes=[
            pltpu.VMEM(TOKEN, BF16),
            pltpu.VMEM((4, TOKENS, 256), BF16),
            pltpu.VMEM((4, TOKENS, 128), BF16),
            pltpu.VMEM((2, TOKENS, 256), BF16),
            pltpu.VMEM((TOKENS, HIDDEN), BF16),
            pltpu.VMEM((TOKENS, HIDDEN), BF16),
        ],
        compiler_params=params(FRONT_MB),
        cost_estimate=pl.CostEstimate(flops=5_000_000_000, bytes_accessed=12_000_000, transcendentals=600_000),
        name="front",
    )(core, *counts, *sectors, w_qkv, w_out, w_up, w_down, cot, *near)


def run_back(core, saved):
    outs = [
        shape((16, 64, 384), BF16),
        shape((4, TOKENS, 128), BF16),
        shape((4, 4 * TOKENS, 128), BF16),
        shape((4, 4 * TOKENS, 128), BF16),
    ]
    return pl.pallas_call(
        back_kernel,
        out_shape=outs,
        in_specs=smem(1) + vmem(len(saved)),
        out_specs=vmem(len(outs)),
        scratch_shapes=[pltpu.VMEM((6, GROUP, KEYS), BF16)],
        compiler_params=params(BACK_MB),
        cost_estimate=pl.CostEstimate(flops=6_000_000_000, bytes_accessed=12_000_000, transcendentals=0),
        name="back",
    )(core, *saved)


def run_push(core, w_qkv, grads, normed):
    outs = [shape((16, 64, 384), BF16), shape((2,) + TOKEN, BF16), shape(TOKEN, BF16), shape(TOKEN, F32)]
    return pl.pallas_call(
        push_kernel,
        out_shape=outs,
        in_specs=smem(1) + vmem(8),
        out_specs=vmem(4),
        compiler_params=params(BACK_MB),
        cost_estimate=pl.CostEstimate(flops=2_000_000_000, bytes_accessed=4_000_000, transcendentals=0),
        name="push",
    )(core, w_qkv, *grads, *normed)


def small_call(kernel, outs, scalars, arrays, name):
    return pl.pallas_call(
        kernel,
        out_shape=outs,
        in_specs=smem(len(scalars)) + vmem(len(arrays)),
        out_specs=vmem(len(outs)),
        compiler_params=params(NEAR_MB),
        cost_estimate=pl.CostEstimate(flops=1_000_000, bytes_accessed=4_000_000, transcendentals=0),
        name=name,
    )(*scalars, *arrays)


def run_join(keep1, recv1, keep2, recv2, after):
    return pl.pallas_call(
        join_kernel,
        out_shape=shape((16, 64, 1024), BF16),
        in_specs=vmem(4) + [pl.BlockSpec(memory_space=pl.ANY)],
        out_specs=vmem(1)[0],
        compiler_params=params(NEAR_MB),
        cost_estimate=pl.CostEstimate(flops=1_000_000, bytes_accessed=4_000_000, transcendentals=0),
        name="join",
    )(keep1, recv1, keep2, recv2, after)


def run_add_x(*parts):
    return small_call(add_x_kernel, [shape(TOKEN, BF16)], [], parts, "add_x")[0]


def run_sum(parts):
    return small_call(sum_kernel, [shape((64, 1024), BF16)], [], [parts], "plane_sum")[0]


def run_finish(*parts):
    return small_call(finish_kernel, [shape(TOKEN, BF16), shape((8, 128), F32)], [], parts, "finish")


def run_final(lon, after, parts):
    outs = [shape((8, 1536), F32), shape((8, 512), F32), shape((8, 1024), F32), shape((16, 512), F32)]
    return pl.pallas_call(
        final_kernel,
        out_shape=outs,
        in_specs=smem(1) + vmem(5),
        out_specs=vmem(len(outs)),
        compiler_params=params(NEAR_MB),
        cost_estimate=pl.CostEstimate(flops=1_000_000, bytes_accessed=400_000, transcendentals=0),
        name="final",
    )(lon, after, *parts)


def sum_sources(values):
    return jnp.sum(values.astype(F32), axis=0).astype(BF16)


def swap(values):
    return lax.ppermute(values, "lon", CORE)


def local(tokens, ocean_count, w_qkv, w_out, w_up, w_down, cotangent):
    flat = tokens.reshape(TOKEN)
    cot = cotangent.reshape(TOKEN)
    tok2 = lax.ppermute(flat, "lon", X_LO)
    count = ocean_count.reshape(1, ROWS_DEV)
    count2 = lax.ppermute(count, "lon", X_LO)
    count1 = swap(count)
    lon = lax.axis_index("lon")
    core = (lon % 2).reshape(1)
    tok1 = swap(flat)
    query, inv_q, *own_kv = run_near(flat, w_qkv)
    tok3 = swap(tok2)
    grad_active = run_active(count, w_down, cot)
    pair = run_pair(tok1, tok2, w_qkv)
    mate_kv, across_kv = pair[:4], pair[4:]
    count3 = swap(count2)
    front = run_front(
        core,
        (count, count1, count2, count3),
        (flat, tok3),
        w_qkv,
        w_out,
        w_up,
        w_down,
        cot,
        (query, *own_kv[1:3], *mate_kv[1:3], *across_kv[1:3], grad_active),
    )
    block_out, keep1, send1, grad_middle = front[:4]
    recv1 = swap(send1)
    saved = [query, inv_q] + [*own_kv, *mate_kv, *across_kv, *front[4:]]
    send2, *grads = run_back(core, saved)
    recv2 = swap(send2)
    normed = [own_kv[0], mate_kv[0], across_kv[0], front[4]]
    keep2, for_core, for_x, grad_own = run_push(core, w_qkv, grads, normed)
    joined = run_join(keep1, recv1, keep2, recv2, for_x)
    plane = lax.all_to_all(joined, ("lat", "lon"), 0, 0, axis_index_groups=PLANE_GROUPS, tiled=True)
    plane, for_x, for_core = lax.optimization_barrier((run_sum(plane), for_x, for_core))
    recv_core = swap(for_core)
    from_x = lax.ppermute(run_add_x(for_x, recv_core), "lon", X_LO)
    column = sum_sources(
        lax.all_to_all(plane.reshape(8, 8, 1024), "lat", 0, 0, axis_index_groups=Z_GROUPS, tiled=True)
    )
    gathered = [column] + [lax.ppermute(column, "lon", table) for table in (CORE, X_LO, DIAGONAL)]
    grad_tokens, done = run_finish(flat, grad_own, recv_core, from_x, grad_middle)
    weights = run_final(lon.reshape(1), done, gathered)
    return (block_out.reshape(tokens.shape), grad_tokens.reshape(tokens.shape), *weights)


def solution(mesh):
    in_specs = (P("lat", "lon", None), P("lat", "lon"), P(), P(), P(), P(), P("lat", "lon", None))
    out_specs = (
        P("lat", "lon", None),
        P("lat", "lon", None),
        P("lat", None),
        P("lat", None),
        P("lat", None),
        P("lat", None),
    )
    return jax.shard_map(local, mesh=mesh, in_specs=in_specs, out_specs=out_specs, check_vma=False)
```

```python
import math

import jax
import jax.numpy as jnp
from jax import lax
from jax.experimental import pallas as pl
from jax.experimental.pallas import tpu as pltpu
from jax.sharding import PartitionSpec as P

F32 = jnp.float32
BF16 = jnp.bfloat16
HEAD_DIM = 64
SOFTMAX_SCALE = 8.0
WIDTH = 512
HIDDEN = 1024
ROWS_DEV = 3
SECTOR = 64
TOKENS = ROWS_DEV * SECTOR
KEYS = 4 * SECTOR
GROUP = 256
GELU_A = math.sqrt(2.0 / math.pi)
GELU_B = 0.044715
NEAR_MB = 20
FRONT_MB = 28
BACK_MB = 28


def lat_index(z, y, x_hi):
    return (z * 4 + y) * 2 + x_hi


CORE = [(0, 1), (1, 0), (2, 3), (3, 2)]
X_LO = [(0, 2), (2, 0), (1, 3), (3, 1)]
DIAGONAL = [(0, 3), (3, 0), (1, 2), (2, 1)]
Z_ORDER = (4, 3, 5, 2, 6, 1, 7, 0)
Z_GROUPS = [[lat_index(z, y, x) for z in Z_ORDER] for y in range(4) for x in range(2)]
FOLDED = (2, 1, 3, 0)
PLANE_ORDER = [y * 4 + x for y in FOLDED for x in FOLDED]
PLANE_GROUPS = [
    [lat_index(z, at // 4, at % 4 // 2) * 4 + at % 2 * 2 + core for at in PLANE_ORDER]
    for z in range(8)
    for core in range(2)
]


def mm(left, right):
    return lax.dot_general(left, right, (((1,), (0,)), ((), ())), preferred_element_type=F32)


def mm_nt(left, right):
    return lax.dot_general(left, right, (((1,), (1,)), ((), ())), preferred_element_type=F32)


def mm_tn(left, right):
    return lax.dot_general(left, right, (((0,), (0,)), ((), ())), preferred_element_type=F32)


def mean_last(values):
    return jnp.sum(values, axis=-1, keepdims=True) * (1.0 / values.shape[-1])


def layer_norm(values):
    centered = values - mean_last(values)
    inverse = lax.rsqrt(mean_last(centered * centered) + 1e-05)
    return centered * inverse, inverse


def layer_norm_back(normed, inverse, grad):
    return inverse * (grad - mean_last(grad) - normed * mean_last(grad * normed))


def head_blocks():
    same = lax.broadcasted_iota(jnp.int32, (GROUP, GROUP), 0) // HEAD_DIM == (
        lax.broadcasted_iota(jnp.int32, (GROUP, GROUP), 1) // HEAD_DIM
    )
    return jnp.where(same, 1.0, 0.0).astype(BF16)


def head_mean(values, blocks):
    parts = [
        mm(values[:, at : at + GROUP].astype(BF16), blocks) for at in range(0, values.shape[1], GROUP)
    ]
    return (parts[0] if len(parts) == 1 else jnp.concatenate(parts, axis=1)) * (1.0 / HEAD_DIM)


def head_masks(dtype):
    lane = lax.broadcasted_iota(jnp.int32, (1, GROUP), 1) // HEAD_DIM
    return [jnp.where(lane == head, 1.0, 0.0).astype(dtype) for head in range(4)]


def stack_heads(values, masks):
    return jnp.concatenate([values * mask for mask in masks], axis=0)


def unstack_heads(values, masks):
    return sum(values[head * SECTOR : (head + 1) * SECTOR] * masks[head] for head in range(4))


def store_pieces(out_ref, x_lo, column, product):
    width = product.shape[1]
    split = product.reshape(8, 8, 8, width)
    for place in range(8):
        piece = jnp.concatenate([split[z, place] for z in Z_ORDER], axis=0)
        out_ref[PLANE_ORDER.index(place * 2 + x_lo), :, column : column + width] = piece.astype(BF16)


def rows_of(row, width=SECTOR):
    return slice(row * width, (row + 1) * width)


def key_value(tok_refs, w_qkv_ref, blocks, *out_refs):
    tokens = jnp.concatenate([ref[...] for ref in tok_refs], axis=0).astype(F32)
    normed = layer_norm(tokens)[0].astype(BF16)
    key_raw = mm(normed, w_qkv_ref[:, WIDTH : 2 * WIDTH])
    value = mm(normed, w_qkv_ref[:, 2 * WIDTH :]).astype(BF16)
    inv_k = lax.rsqrt(head_mean(key_raw * key_raw, blocks) + 1e-06)
    made = (normed, (key_raw * inv_k).astype(BF16), value, inv_k.astype(BF16))
    for at, ref in enumerate(out_refs):
        first = at // 4 * TOKENS
        ref[...] = made[at % 4][first : first + TOKENS]
    return normed


def own_mask(count_ref):
    place = lax.broadcasted_iota(jnp.int32, (SECTOR, 1), 0)
    return jnp.concatenate(
        [jnp.where(place < count_ref[0, row], 1.0, 0.0) for row in range(ROWS_DEV)], axis=0
    )


def near_kernel(tok0_ref, w_qkv_ref, query_ref, inv_q_ref, *own_refs):
    blocks = head_blocks()
    normed = key_value([tok0_ref], w_qkv_ref, blocks, *own_refs)
    query_raw = mm(normed, w_qkv_ref[:, :WIDTH])
    inv_q = lax.rsqrt(head_mean(query_raw * query_raw, blocks) + 1e-06)
    inv_q_ref[...] = inv_q.astype(BF16)
    query_ref[...] = (query_raw * inv_q).astype(BF16)


def active_kernel(count_ref, w_down_ref, cot_ref, grad_active_ref):
    branch = (own_mask(count_ref) * cot_ref[...].astype(F32)).astype(BF16)
    grad_active_ref[...] = mm_nt(branch, w_down_ref[...]).astype(BF16)


def pair_kernel(tok1_ref, tok2_ref, w_qkv_ref, *refs):
    key_value([tok1_ref, tok2_ref], w_qkv_ref, head_blocks(), *refs)


PLACES = [(row, slice(low, low + GROUP)) for row in range(ROWS_DEV) for low in (0, GROUP)]


def row_join(row, lanes, refs):
    return jnp.concatenate([ref[rows_of(row), lanes] for ref in refs], axis=0)


def front_kernel(
    core_ref,
    count_ref,
    count1_ref,
    count2_ref,
    count3_ref,
    tok0_ref,
    tok3_ref,
    w_qkv_ref,
    w_out_ref,
    w_up_ref,
    w_down_ref,
    cot_ref,
    query_ref,
    own_key_ref,
    own_value_ref,
    mate_key_ref,
    mate_value_ref,
    across_key_ref,
    across_value_ref,
    grad_active_ref,
    block_out_ref,
    keep_ref,
    send_ref,
    grad_middle_ref,
    normed_ref,
    key_ref,
    value_ref,
    inv_k_ref,
    probs_ref,
    grad_att_ref,
    att_ref,
    lift_ref,
    attn_ref,
    branch_ref,
    active_ref,
    glift_ref,
):
    blocks = head_blocks()
    masks_b = head_masks(BF16)
    masks_f = head_masks(F32)
    core = core_ref[0]
    key_value([tok3_ref], w_qkv_ref, blocks, normed_ref, key_ref, value_ref, inv_k_ref)
    key_refs = (own_key_ref, mate_key_ref, across_key_ref, key_ref)
    value_refs = (own_value_ref, mate_value_ref, across_value_ref, value_ref)

    key_place = lax.broadcasted_iota(jnp.int32, (1, KEYS), 1)
    key_masks = []
    for row in range(ROWS_DEV):
        limit = jnp.zeros((1, KEYS), jnp.int32)
        for sector, ref in enumerate((count_ref, count1_ref, count2_ref, count3_ref)):
            limit = jnp.where(key_place // SECTOR == sector, ref[0, row], limit)
        key_masks.append(jnp.where(key_place % SECTOR < limit, 1.0, 0.0))
    scores = [
        mm_nt(stack_heads(query_ref[rows_of(row), lanes], masks_b), row_join(row, lanes, key_refs))
        for row, lanes in PLACES
    ]
    for at, (row, lanes) in enumerate(PLACES):
        for head in range(4):
            some = rows_of(head)
            logits = scores[at][some] * (SOFTMAX_SCALE / HEAD_DIM) - SOFTMAX_SCALE
            expscore = jnp.exp(logits) * key_masks[row]
            total = jnp.sum(expscore, axis=1, keepdims=True)
            probs_ref[at, some, :] = (expscore * (1.0 / total)).astype(BF16)
    mixed = [mm(probs_ref[at], row_join(row, lanes, value_refs)) for at, (row, lanes) in enumerate(PLACES)]
    for at, (row, lanes) in enumerate(PLACES):
        att_ref[rows_of(row), lanes] = unstack_heads(mixed[at], masks_f).astype(BF16)

    mask = own_mask(count_ref)
    attended = att_ref[...]
    middle = tok0_ref[...].astype(F32) + mask * mm(attended, w_out_ref[...])
    normed_two, inverse = layer_norm(middle)
    normed_two_b = normed_two.astype(BF16)
    lifted = mm(normed_two_b, w_up_ref[...])
    for low in range(0, TOKENS, 48):
        rows = slice(low, low + 48)
        some = lifted[rows]
        square = some * some
        bent = jnp.tanh(GELU_A * some * (1.0 + GELU_B * square))
        half = 0.5 * (1.0 + bent)
        active_ref[rows, :] = (some * half).astype(BF16)
        slope = half + 0.5 * some * (1.0 - bent * bent) * (GELU_A * (1.0 + 3.0 * GELU_B * square))
        glift_ref[rows, :] = (slope * grad_active_ref[rows, :].astype(F32)).astype(BF16)
    active, grad_lifted = active_ref[...], glift_ref[...]
    branch = (mask * cot_ref[...].astype(F32)).astype(BF16)
    grad_normed = mm_nt(grad_lifted, w_up_ref[...])
    for part in range(2):
        branch_ref[part] = branch[:, part * 256 : (part + 1) * 256]
    for part in range(4):
        lift_ref[part] = grad_lifted[:, part * 256 : (part + 1) * 256]
    halves = ((keep_ref, core), (send_ref, 1 - core))
    active_t, normed_two_t = active.T, normed_two_b.T
    for out_ref, half_index in halves:
        term_down = mm(active_t, branch_ref[half_index]).reshape(64, 2, 8, 256)
        for x_lo in range(2):
            store_pieces(out_ref, x_lo, 384, term_down[:, x_lo].reshape(512, 256))
    grad_middle = cot_ref[...].astype(F32) + layer_norm_back(normed_two, inverse, grad_normed)
    grad_middle_ref[...] = grad_middle
    grad_attn = (mask * grad_middle).astype(BF16)
    grad_att_ref[...] = mm_nt(grad_attn, w_out_ref[...]).astype(BF16)
    block_out_ref[...] = (middle + mask * mm(active, w_down_ref[...])).astype(BF16)
    for out_ref, half_index in halves:
        for x_lo in range(2):
            store_pieces(out_ref, x_lo, 128, mm(normed_two_t, lift_ref[half_index + 2 * x_lo]))
    for part in range(4):
        attn_ref[part] = grad_attn[:, part * 128 : (part + 1) * 128]
    attended_t = attended.T
    for out_ref, half_index in halves:
        pair = jnp.concatenate([attn_ref[half_index], attn_ref[half_index + 2]], axis=1)
        term_out = mm(attended_t, pair)
        for x_lo in range(2):
            store_pieces(out_ref, x_lo, 0, term_out[:, x_lo * 128 : (x_lo + 1) * 128])


def norm_back(normed_b, inverse_b, grad, blocks):
    normed = normed_b.astype(F32)
    shift = head_mean(normed * grad, blocks)
    return (inverse_b.astype(F32) * (grad - normed * shift)).astype(BF16)


def qkv_half(out_ref, half_index, normed_refs, gq_ref, gk_ref, gv_ref):
    normed_all = jnp.concatenate([ref[...] for ref in normed_refs], axis=0)
    own_normed_t, normed_all_t = normed_refs[0][...].T, normed_all.T
    pair = jnp.concatenate([gq_ref[half_index], gq_ref[half_index + 2]], axis=1)
    term_q = mm(own_normed_t, pair)
    for x_lo in range(2):
        store_pieces(out_ref, x_lo, 0, term_q[:, x_lo * 128 : (x_lo + 1) * 128])
        pair = jnp.concatenate([gk_ref[half_index + 2 * x_lo], gv_ref[half_index + 2 * x_lo]], axis=1)
        store_pieces(out_ref, x_lo, 128, mm(normed_all_t, pair))


def back_kernel(core_ref, query_ref, inv_q_ref, *refs):
    sectors, (probs_ref, grad_att_ref, send_ref, gq_ref, gk_ref, gv_ref, scores_ref) = refs[:16], refs[16:]
    normed_refs, key_refs, value_refs, inv_k_refs = (sectors[at::4] for at in range(4))
    blocks = head_blocks()
    masks_b = head_masks(BF16)
    masks_f = head_masks(F32)
    stacked_q = [stack_heads(query_ref[rows_of(row), lanes], masks_b) for row, lanes in PLACES]
    stacked_g = [stack_heads(grad_att_ref[rows_of(row), lanes], masks_b) for row, lanes in PLACES]
    keys = [row_join(row, lanes, key_refs) for row, lanes in PLACES]
    grad_probs = [
        mm_nt(stacked_g[at], row_join(row, lanes, value_refs)) for at, (row, lanes) in enumerate(PLACES)
    ]
    for at in range(len(PLACES)):
        for head in range(4):
            some = rows_of(head)
            probs = probs_ref[at, some, :].astype(F32)
            grads = grad_probs[at][some]
            delta = jnp.sum(probs * grads, axis=1, keepdims=True)
            scores_ref[at, some, :] = (probs * (grads - delta) * (SOFTMAX_SCALE / HEAD_DIM)).astype(BF16)
    grad_scores = [scores_ref[at] for at in range(len(PLACES))]
    grad_v = [mm_tn(probs_ref[at], stacked_g[at]).astype(BF16) for at in range(len(PLACES))]
    grad_k = [mm_tn(grad_scores[at], stacked_q[at]) for at in range(len(PLACES))]
    grad_q = [unstack_heads(mm(grad_scores[at], keys[at]), masks_f) for at in range(len(PLACES))]
    for at, (row, lanes) in enumerate(PLACES):
        own = rows_of(row)
        back_q = norm_back(query_ref[own, lanes], inv_q_ref[own, lanes], grad_q[at], blocks)
        back_k = norm_back(keys[at], row_join(row, lanes, inv_k_refs), grad_k[at], blocks)
        for part in range(2):
            cut = slice(part * 128, (part + 1) * 128)
            quarter = lanes.start // 128 + part
            gq_ref[quarter, own, :] = back_q[:, cut]
            for ref, grad in ((gk_ref, back_k), (gv_ref, grad_v[at])):
                for sector in range(4):
                    rows = slice(sector * TOKENS + own.start, sector * TOKENS + own.stop)
                    ref[quarter, rows, :] = grad[sector * SECTOR : (sector + 1) * SECTOR, cut]

    qkv_half(send_ref, 1 - core_ref[0], normed_refs, gq_ref, gk_ref, gv_ref)


def push_kernel(core_ref, w_qkv_ref, gq_ref, gk_ref, gv_ref, *refs):
    normed_refs, (keep_ref, for_core_ref, for_x_ref, own_ref) = refs[:4], refs[4:]
    grad_q = jnp.concatenate([gq_ref[part] for part in range(4)], axis=1)
    grad_kv = jnp.concatenate([ref[part] for ref in (gk_ref, gv_ref) for part in range(4)], axis=1)
    grad_normed = mm_nt(grad_kv, w_qkv_ref[:, WIDTH:])
    for_core_ref[0] = grad_normed[TOKENS : 2 * TOKENS].astype(BF16)
    for_x_ref[...] = grad_normed[2 * TOKENS : 3 * TOKENS].astype(BF16)
    for_core_ref[1] = grad_normed[3 * TOKENS :].astype(BF16)
    own_ref[...] = grad_normed[:TOKENS] + mm_nt(grad_q, w_qkv_ref[:, :WIDTH])
    qkv_half(keep_ref, core_ref[0], normed_refs, gq_ref, gk_ref, gv_ref)


def join_kernel(keep1_ref, recv1_ref, keep2_ref, recv2_ref, after_ref, out_ref):
    del after_ref
    for piece in range(16):
        out_ref[piece, :, :384] = (keep2_ref[piece].astype(F32) + recv2_ref[piece].astype(F32)).astype(BF16)
        out_ref[piece, :, 384:] = (keep1_ref[piece].astype(F32) + recv1_ref[piece].astype(F32)).astype(BF16)


def add_x_kernel(for_x_ref, recv_core_ref, out_ref):
    out_ref[...] = (for_x_ref[...].astype(F32) + recv_core_ref[1].astype(F32)).astype(BF16)


def sum_kernel(parts_ref, out_ref):
    for low in range(0, out_ref.shape[0], 16):
        rows = slice(low, low + 16)
        total = parts_ref[0, rows, :].astype(F32)
        for part in range(1, parts_ref.shape[0]):
            total = total + parts_ref[part, rows, :].astype(F32)
        out_ref[rows, :] = total.astype(BF16)


def finish_kernel(tok_ref, own_ref, recv_core_ref, from_x_ref, middle_ref, out_ref, done_ref):
    done_ref[...] = jnp.zeros((8, 128), F32)
    grad = own_ref[...] + recv_core_ref[0].astype(F32) + from_x_ref[...].astype(F32)
    normed, inverse = layer_norm(tok_ref[...].astype(F32))
    out_ref[...] = (middle_ref[...] + layer_norm_back(normed, inverse, grad)).astype(BF16)


def final_kernel(lon_ref, after_ref, own_ref, core_ref, x_ref, diagonal_ref, qkv_ref, out_ref, up_ref, down_ref):
    del after_ref
    lon = lon_ref[0]
    scale = 1.0 / math.sqrt(64 * 4 * TOKENS)
    held = [ref[...].astype(F32) * scale for ref in (own_ref, core_ref, x_ref, diagonal_ref)]
    for quarter in range(4):
        part = held[3]
        for distance in range(3):
            part = jnp.where(lon == (quarter ^ distance), held[distance], part)
        at = slice(quarter * 128, (quarter + 1) * 128)
        for matrix in range(3):
            low = matrix * WIDTH + quarter * 128
            qkv_ref[:, low : low + 128] = part[:, matrix * 128 : (matrix + 1) * 128]
        out_ref[:, at] = part[:, 384:512]
        up_ref[:, quarter * 256 : (quarter + 1) * 256] = part[:, 512:768]
        side = (quarter % 2) * 256
        down_ref[(quarter // 2) * 8 : (quarter // 2) * 8 + 8, side : side + 256] = part[:, 768:]


def vmem(count):
    return [pl.BlockSpec(memory_space=pltpu.VMEM)] * count


def smem(count):
    return [pl.BlockSpec(memory_space=pltpu.SMEM)] * count


def shape(dims, dtype):
    return jax.ShapeDtypeStruct(dims, dtype)


TOKEN = (TOKENS, WIDTH)


def params(megabytes):
    return pltpu.CompilerParams(vmem_limit_bytes=megabytes * 1024 * 1024)


def run_near(tok0, w_qkv):
    outs = [shape(TOKEN, BF16)] * 6
    return pl.pallas_call(
        near_kernel,
        out_shape=outs,
        in_specs=vmem(2),
        out_specs=vmem(len(outs)),
        compiler_params=params(NEAR_MB),
        cost_estimate=pl.CostEstimate(flops=2_500_000_000, bytes_accessed=4_000_000, transcendentals=0),
        name="near",
    )(tok0, w_qkv)


def run_active(count, w_down, cot):
    return pl.pallas_call(
        active_kernel,
        out_shape=shape((TOKENS, HIDDEN), BF16),
        in_specs=smem(1) + vmem(2),
        out_specs=vmem(1)[0],
        compiler_params=params(NEAR_MB),
        cost_estimate=pl.CostEstimate(flops=2_500_000_000, bytes_accessed=2_000_000, transcendentals=0),
        name="active",
    )(count, w_down, cot)


def run_pair(tok1, tok2, w_qkv):
    outs = [shape(TOKEN, BF16)] * 8
    return pl.pallas_call(
        pair_kernel,
        out_shape=outs,
        in_specs=vmem(3),
        out_specs=vmem(len(outs)),
        compiler_params=params(NEAR_MB),
        cost_estimate=pl.CostEstimate(flops=20_000_000_000, bytes_accessed=2_000_000, transcendentals=0),
        name="pair",
    )(tok1, tok2, w_qkv)


def run_front(core, counts, sectors, w_qkv, w_out, w_up, w_down, cot, near):
    outs = [
        shape(TOKEN, BF16),
        shape((16, 64, 640), BF16),
        shape((16, 64, 640), BF16),
        shape(TOKEN, F32),
        shape(TOKEN, BF16),
        shape(TOKEN, BF16),
        shape(TOKEN, BF16),
        shape(TOKEN, BF16),
        shape((6, GROUP, KEYS), BF16),
        shape(TOKEN, BF16),
    ]
    return pl.pallas_call(
        front_kernel,
        out_shape=outs,
        in_specs=smem(5) + vmem(7 + len(near)),
        out_specs=vmem(len(outs)),
        scratch_shapes=[
            pltpu.VMEM(TOKEN, BF16),
            pltpu.VMEM((4, TOKENS, 256), BF16),
            pltpu.VMEM((4, TOKENS, 128), BF16),
            pltpu.VMEM((2, TOKENS, 256), BF16),
            pltpu.VMEM((TOKENS, HIDDEN), BF16),
            pltpu.VMEM((TOKENS, HIDDEN), BF16),
        ],
        compiler_params=params(FRONT_MB),
        cost_estimate=pl.CostEstimate(flops=5_000_000_000, bytes_accessed=12_000_000, transcendentals=600_000),
        name="front",
    )(core, *counts, *sectors, w_qkv, w_out, w_up, w_down, cot, *near)


def run_back(core, saved):
    outs = [
        shape((16, 64, 384), BF16),
        shape((4, TOKENS, 128), BF16),
        shape((4, 4 * TOKENS, 128), BF16),
        shape((4, 4 * TOKENS, 128), BF16),
    ]
    return pl.pallas_call(
        back_kernel,
        out_shape=outs,
        in_specs=smem(1) + vmem(len(saved)),
        out_specs=vmem(len(outs)),
        scratch_shapes=[pltpu.VMEM((6, GROUP, KEYS), BF16)],
        compiler_params=params(BACK_MB),
        cost_estimate=pl.CostEstimate(flops=6_000_000_000, bytes_accessed=12_000_000, transcendentals=0),
        name="back",
    )(core, *saved)


def run_push(core, w_qkv, grads, normed):
    outs = [shape((16, 64, 384), BF16), shape((2,) + TOKEN, BF16), shape(TOKEN, BF16), shape(TOKEN, F32)]
    return pl.pallas_call(
        push_kernel,
        out_shape=outs,
        in_specs=smem(1) + vmem(8),
        out_specs=vmem(4),
        compiler_params=params(BACK_MB),
        cost_estimate=pl.CostEstimate(flops=2_000_000_000, bytes_accessed=4_000_000, transcendentals=0),
        name="push",
    )(core, w_qkv, *grads, *normed)


def small_call(kernel, outs, scalars, arrays, name):
    return pl.pallas_call(
        kernel,
        out_shape=outs,
        in_specs=smem(len(scalars)) + vmem(len(arrays)),
        out_specs=vmem(len(outs)),
        compiler_params=params(NEAR_MB),
        cost_estimate=pl.CostEstimate(flops=1_000_000, bytes_accessed=4_000_000, transcendentals=0),
        name=name,
    )(*scalars, *arrays)


def run_join(keep1, recv1, keep2, recv2, after):
    return pl.pallas_call(
        join_kernel,
        out_shape=shape((16, 64, 1024), BF16),
        in_specs=vmem(4) + [pl.BlockSpec(memory_space=pl.ANY)],
        out_specs=vmem(1)[0],
        compiler_params=params(NEAR_MB),
        cost_estimate=pl.CostEstimate(flops=1_000_000, bytes_accessed=4_000_000, transcendentals=0),
        name="join",
    )(keep1, recv1, keep2, recv2, after)


def run_add_x(*parts):
    return small_call(add_x_kernel, [shape(TOKEN, BF16)], [], parts, "add_x")[0]


def run_sum(parts):
    return small_call(sum_kernel, [shape((64, 1024), BF16)], [], [parts], "plane_sum")[0]


def run_finish(*parts):
    return small_call(finish_kernel, [shape(TOKEN, BF16), shape((8, 128), F32)], [], parts, "finish")


def run_final(lon, after, parts):
    outs = [shape((8, 1536), F32), shape((8, 512), F32), shape((8, 1024), F32), shape((16, 512), F32)]
    return pl.pallas_call(
        final_kernel,
        out_shape=outs,
        in_specs=smem(1) + vmem(5),
        out_specs=vmem(len(outs)),
        compiler_params=params(NEAR_MB),
        cost_estimate=pl.CostEstimate(flops=1_000_000, bytes_accessed=400_000, transcendentals=0),
        name="final",
    )(lon, after, *parts)


def sum_sources(values):
    return jnp.sum(values.astype(F32), axis=0).astype(BF16)


def swap(values):
    return lax.ppermute(values, "lon", CORE)


def local(tokens, ocean_count, w_qkv, w_out, w_up, w_down, cotangent):
    flat = tokens.reshape(TOKEN)
    cot = cotangent.reshape(TOKEN)
    tok2 = lax.ppermute(flat, "lon", X_LO)
    count = ocean_count.reshape(1, ROWS_DEV)
    count2 = lax.ppermute(count, "lon", X_LO)
    count1 = swap(count)
    lon = lax.axis_index("lon")
    core = (lon % 2).reshape(1)
    tok1 = swap(flat)
    query, inv_q, *own_kv = run_near(flat, w_qkv)
    tok3 = swap(tok2)
    grad_active = run_active(count, w_down, cot)
    pair = run_pair(tok1, tok2, w_qkv)
    mate_kv, across_kv = pair[:4], pair[4:]
    count3 = swap(count2)
    front = run_front(
        core,
        (count, count1, count2, count3),
        (flat, tok3),
        w_qkv,
        w_out,
        w_up,
        w_down,
        cot,
        (query, *own_kv[1:3], *mate_kv[1:3], *across_kv[1:3], grad_active),
    )
    block_out, keep1, send1, grad_middle = front[:4]
    recv1 = swap(send1)
    saved = [query, inv_q] + [*own_kv, *mate_kv, *across_kv, *front[4:]]
    send2, *grads = run_back(core, saved)
    recv2 = swap(send2)
    normed = [own_kv[0], mate_kv[0], across_kv[0], front[4]]
    keep2, for_core, for_x, grad_own = run_push(core, w_qkv, grads, normed)
    joined = run_join(keep1, recv1, keep2, recv2, for_x)
    plane = lax.all_to_all(joined, ("lat", "lon"), 0, 0, axis_index_groups=PLANE_GROUPS, tiled=True)
    plane, for_x, for_core = lax.optimization_barrier((run_sum(plane), for_x, for_core))
    recv_core = swap(for_core)
    from_x = lax.ppermute(run_add_x(for_x, recv_core), "lon", X_LO)
    column = sum_sources(
        lax.all_to_all(plane.reshape(8, 8, 1024), "lat", 0, 0, axis_index_groups=Z_GROUPS, tiled=True)
    )
    gathered = [column] + [lax.ppermute(column, "lon", table) for table in (CORE, X_LO, DIAGONAL)]
    grad_tokens, done = run_finish(flat, grad_own, recv_core, from_x, grad_middle)
    weights = run_final(lon.reshape(1), done, gathered)
    return (block_out.reshape(tokens.shape), grad_tokens.reshape(tokens.shape), *weights)


def solution(mesh):
    in_specs = (P("lat", "lon", None), P("lat", "lon"), P(), P(), P(), P(), P("lat", "lon", None))
    out_specs = (
        P("lat", "lon", None),
        P("lat", "lon", None),
        P("lat", None),
        P("lat", None),
        P("lat", None),
        P("lat", None),
    )
    return jax.shard_map(local, mesh=mesh, in_specs=in_specs, out_specs=out_specs, check_vma=False)
```
